32 devices in a mesh: xg: 4 (over z), yd: 8 (over y, x, core).
Axes of the slice: x: 2, y: 2, z: 4, core: 2. Of those that a mesh axis runs over, the one named last changes fastest.
Arguments:
- cotangent: float32 [2, 1, 2048, 1024], P(None, None, 'xg', 'yd'), may hold values from -240 to 240
- x_diffusivity: float32 [2, 1, 2048, 1024], P(None, None, 'xg', 'yd'), may hold values from 0.05 to 2
- x_speed: float32 [1, 2048, 1024], P(None, 'xg', 'yd'), may hold values from 1024 to 8192
- x_upwind: int32 [1, 2048, 1024], P(None, 'xg', 'yd'), may hold values from 0 to 1
- y_diffusivity: float32 [2, 1, 2048, 1024], P(None, None, 'xg', 'yd'), may hold values from 64 to 2048
- y_speed: float32 [1, 2048, 1024], P(None, 'xg', 'yd'), may hold values from 1024 to 8192
- y_upwind: int32 [1, 2048, 1024], P(None, 'xg', 'yd'), may hold values from 0 to 1
- coupling: float32 [4, 1, 2048, 1024], P(None, None, 'xg', 'yd'), may hold values from -1.8 to 2, as said below
- x_codes: int32 [1, 1024], P(None, 'yd'), may hold values from 0 to 2
- y_codes: int32 [1, 2048], P(None, 'xg'), may hold values from 0 to 2
Outputs:
- state_grad: float32 [2, 1, 2048, 1024], P(None, None, 'xg', 'yd')
The draws below stay inside these ranges and needn't reach their ends.
Inputs may be any that keep to these rules, and one draw needn't show every extreme that they name: `coupling`: coupling_0 and coupling_3 lie in 0.01 to 2; |coupling_2| is at most 0.9 coupling_0 and |coupling_1| at most 0.9 coupling_3.
All inputs are finite; a program needn't handle non-finite values.
Results may differ from the reference program's by a relative error of at most 0.0003.
Values sent between devices are 32-bit elements; how exact they have to be, the bound alone decides.
A program may use at most 128 MiB of HBM per device.

```python
import math
import jax
import jax.numpy as jnp
from jax import lax

LEV = 1
NX = 2048
NY = 1024


def draw_cotangent(key, part):
    shape = (2, LEV, NX, NY)
    keys = jax.random.split(jax.random.fold_in(key, 11), 5)
    wave_x = jax.random.randint(keys[0], (2, LEV, 1, 1), 1, 5).astype(jnp.float32)
    wave_y = jax.random.randint(keys[1], (2, LEV, 1, 1), 1, 5).astype(jnp.float32)
    phases = jax.random.uniform(keys[2], (2, 2, LEV, 1, 1), jnp.float32, 0.0, 6.2831853)
    cell_x = lax.broadcasted_iota(jnp.float32, (1, 1, NX, 1), 2) / NX
    cell_y = lax.broadcasted_iota(jnp.float32, (1, 1, 1, NY), 3) / NY
    smooth = jnp.cos(6.2831853 * wave_x * cell_x + phases[0]) * jnp.cos(6.2831853 * wave_y * cell_y + phases[1])
    values = jnp.clip(48.0 * jax.random.normal(keys[4], shape, jnp.float32) + 16.0 * smooth, -240.0, 240.0)
    return values


def coherent_runs(key, lines_shape, full_shape, length, axis_dim, flip_every):
    keys = jax.random.split(key, 4)
    heading = jax.random.randint(keys[0], lines_shape, 0, 2)
    run_start = jax.random.randint(keys[1], lines_shape, 0, length)
    if flip_every > 0:
        run_length = jax.random.randint(keys[2], lines_shape, 1, length // 4 + 1)
    else:
        run_length = jax.random.randint(keys[2], lines_shape, max(length // 32, 1), length // 4 + 1)
    position = lax.broadcasted_iota(jnp.int32, full_shape, axis_dim)
    inside = (position >= run_start) & (position < run_start + run_length)
    flows = jnp.where(inside, 1 - heading, heading)
    if flip_every > 0:
        single = jax.random.randint(keys[3], full_shape, 0, flip_every) == 0
        flows = jnp.where(single, 1 - flows, flows)
    return flows.astype(jnp.int32)


def draw_x_upwind(key, part):
    return coherent_runs(jax.random.fold_in(key, 21), (LEV, 1, NY), (LEV, NX, NY), NX, 1, 48)


def draw_y_upwind(key, part):
    return coherent_runs(jax.random.fold_in(key, 31), (LEV, NX, 1), (LEV, NX, NY), NY, 2, 0)


def draw_coupling(key, part):
    keys = jax.random.split(jax.random.fold_in(key, 7), 4)
    shape = (LEV, NX, NY)
    first_diag = jnp.exp(jax.random.uniform(keys[0], shape, jnp.float32, -4.6051702, 0.6931472))
    second_diag = jnp.exp(jax.random.uniform(keys[1], shape, jnp.float32, -4.6051702, 0.6931472))
    first_ratio = jax.random.uniform(keys[2], shape, jnp.float32, -0.9, 0.9)
    second_ratio = jax.random.uniform(keys[3], shape, jnp.float32, -0.9, 0.9)
    first_diag = jnp.clip(first_diag, 0.01, 2.0)
    second_diag = jnp.clip(second_diag, 0.01, 2.0)
    return jnp.stack([first_diag, second_ratio * second_diag, first_ratio * first_diag, second_diag])


def set_ends(entries, own_key, low, high):
    longest = entries.shape.index(max(entries.shape))
    spots = []
    for shift in (0, 1):
        where = [jax.random.randint(jax.random.fold_in(own_key, axis), (), 0, length) for axis, length in enumerate(entries.shape)]
        where[longest] = (where[longest] + shift) % entries.shape[longest]
        spots.append(tuple(where))
    return entries.at[spots[0]].set(low).at[spots[1]].set(high)


def levels(rng, extent, shards, least, top_value):
    factor_of = 1.0
    for axis_at, parts in shards:
        draws = jax.random.uniform(jax.random.fold_in(jax.random.fold_in(rng, 6), axis_at), (parts,), jnp.float32, least / len(shards), top_value / len(shards))
        factor_of = factor_of * jnp.repeat(jnp.exp(draws), extent[axis_at] // parts).reshape((-1,) + (1,) * (len(extent) - 1 - axis_at))
    return factor_of


def setup_inputs(seed: int = 0) -> dict:
    streams_of = jax.random.split(jax.random.key(seed), 11)
    cotangent = draw_cotangent(jax.random.fold_in(streams_of[10], 71), 0)
    x_diffusivity = jnp.clip(jnp.exp(math.log(2.0) - 3.6888794 * jax.random.uniform(streams_of[1], (2, LEV, NX, NY), jnp.float32) ** levels(streams_of[1], (2, LEV, NX, NY), ((2, 4), (3, 8)), -0.2, 0.2)), 0.05, 2.0)
    x_speed = jnp.clip(jnp.exp(math.log(8192.0) - 2.0794415 * jax.random.uniform(streams_of[2], (LEV, NX, NY), jnp.float32) ** levels(streams_of[2], (LEV, NX, NY), ((1, 4), (2, 8)), -0.2, 0.2)), 1024.0, 8192.0)
    x_upwind = draw_x_upwind(jax.random.fold_in(streams_of[10], 71), 0)
    y_diffusivity = jnp.clip(jnp.exp(math.log(2048.0) - 3.465736 * jax.random.uniform(streams_of[4], (2, LEV, NX, NY), jnp.float32) ** levels(streams_of[4], (2, LEV, NX, NY), ((2, 4), (3, 8)), -0.2, 0.2)), 64.0, 2048.0)
    y_speed = jnp.clip(jnp.exp(math.log(8192.0) - 2.0794415 * jax.random.uniform(streams_of[5], (LEV, NX, NY), jnp.float32) ** levels(streams_of[5], (LEV, NX, NY), ((1, 4), (2, 8)), -0.2, 0.2)), 1024.0, 8192.0)
    y_upwind = draw_y_upwind(jax.random.fold_in(streams_of[10], 71), 0)
    coupling = draw_coupling(jax.random.fold_in(streams_of[10], 71), 0)
    x_codes = set_ends(jax.random.randint(streams_of[8], (LEV, NY), 0, 3), jax.random.fold_in(streams_of[8], 1), 0, 2).astype(jnp.int32)
    y_codes = set_ends(jax.random.randint(streams_of[9], (LEV, NX), 0, 3), jax.random.fold_in(streams_of[9], 1), 0, 2).astype(jnp.int32)
    return {"cotangent": cotangent, "x_diffusivity": x_diffusivity, "x_speed": x_speed, "x_upwind": x_upwind, "y_diffusivity": y_diffusivity, "y_speed": y_speed, "y_upwind": y_upwind, "coupling": coupling, "x_codes": x_codes, "y_codes": y_codes}


def face_terms(speed, upwind, diffusivity, codes, first_face):
    flow = upwind.astype(jnp.float32)
    left_coeff = speed * flow + diffusivity
    right_coeff = speed * (1.0 - flow) + diffusivity
    vented = (codes >= 1).astype(jnp.float32)
    opened = (codes == 1).astype(jnp.float32)
    boundary = vented * speed * (1.0 - flow) + opened * diffusivity
    right_coeff = jnp.where(first_face, boundary, right_coeff)
    return left_coeff, right_coeff


def mat_mul(first_mat, second_mat):
    return (first_mat[0] * second_mat[0] + first_mat[1] * second_mat[2],
            first_mat[0] * second_mat[1] + first_mat[1] * second_mat[3],
            first_mat[2] * second_mat[0] + first_mat[3] * second_mat[2],
            first_mat[2] * second_mat[1] + first_mat[3] * second_mat[3])


def mat_vec(matrix, vector):
    return (matrix[0] * vector[0] + matrix[1] * vector[1], matrix[2] * vector[0] + matrix[3] * vector[1])


def mat_inv(matrix):
    determinant = matrix[0] * matrix[3] - matrix[1] * matrix[2]
    return (matrix[3] / determinant, -matrix[1] / determinant, -matrix[2] / determinant, matrix[0] / determinant)


def scalar_sweep(sub_term, main_term, super_term, source, axis_dim):
    items = tuple(jnp.moveaxis(entry, axis_dim, 0) for entry in (sub_term, main_term, super_term, source))

    def forward(carry, item):
        factor, partial_value = carry
        below, centre, above, value = item
        denominator = centre - below * factor
        new_factor = above / denominator
        new_partial = (value - below * partial_value) / denominator
        return (new_factor, new_partial), (new_factor, new_partial)

    start = jnp.zeros_like(items[0][0])
    _, (factors, partials) = lax.scan(forward, (start, start), items)

    def backward(later, item):
        factor, partial_value = item
        current = partial_value - factor * later
        return current, current

    _, solved = lax.scan(backward, start, (factors, partials), reverse=True)
    return jnp.moveaxis(solved, 0, axis_dim)


def block_sweep(lower, middle, upper, values):
    def forward(carry, item):
        factor, partial_value = carry
        below, centre, above, value = item
        reduced = tuple(entry - other for entry, other in zip(centre, mat_mul(below, factor)))
        inverse = mat_inv(reduced)
        new_factor = mat_mul(inverse, above)
        shifted = mat_vec(below, partial_value)
        new_partial = mat_vec(inverse, (value[0] - shifted[0], value[1] - shifted[1]))
        return (new_factor, new_partial), (new_factor, new_partial)

    start = jnp.zeros_like(middle[0][0])
    init = ((start, start, start, start), (start, start))
    _, (factors, partials) = lax.scan(forward, init, (lower, middle, upper, values))

    def backward(later, item):
        factor, partial_value = item
        pushed = mat_vec(factor, later)
        current = (partial_value[0] - pushed[0], partial_value[1] - pushed[1])
        return current, current

    _, solved = lax.scan(backward, (start, start), (factors, partials), reverse=True)
    return solved


def reference(cotangent, x_diffusivity, x_speed, x_upwind, y_diffusivity, y_speed, y_upwind, coupling, x_codes, y_codes):
    x_first = lax.broadcasted_iota(jnp.int32, (1, 1, NX, 1), 2) == 0
    y_first = lax.broadcasted_iota(jnp.int32, (1, 1, 1, NY), 3) == 0
    x_left, x_right = face_terms(x_speed[None], x_upwind[None], x_diffusivity, x_codes[None, :, None, :], x_first)
    y_left, y_right = face_terms(y_speed[None], y_upwind[None], y_diffusivity, y_codes[None, :, :, None], y_first)
    y_ahead = jnp.concatenate([y_left[:, :, :, 1:], jnp.zeros_like(y_left[:, :, :, :1])], axis=3)
    weights = scalar_sweep(-y_right, 1.0 + y_ahead + y_right, -y_ahead, cotangent, 3)
    x_ahead = jnp.concatenate([x_left[:, :, 1:, :], jnp.zeros_like(x_left[:, :, :1, :])], axis=2)
    zero = jnp.zeros_like(x_ahead[0])
    lower = (-x_right[0], zero, zero, -x_right[1])
    middle = (1.0 + x_ahead[0] + x_right[0] + 0.5 * coupling[0], 0.5 * coupling[2], 0.5 * coupling[1],
              1.0 + x_ahead[1] + x_right[1] + 0.5 * coupling[3])
    upper = (-x_ahead[0], zero, zero, -x_ahead[1])
    values = (weights[0], weights[1])
    moved = [tuple(jnp.moveaxis(entry, 1, 0) for entry in group) for group in (lower, middle, upper, values)]
    solved = block_sweep(moved[0], moved[1], moved[2], moved[3])
    return jnp.stack([jnp.moveaxis(entry, 0, 1) for entry in solved])
```

```python
import functools

import jax
import jax.numpy as jnp
from jax import lax
from jax.experimental import pallas as pl
from jax.experimental.pallas import tpu as pltpu
from jax.sharding import PartitionSpec as P

LANES = 128
SUB = 8
F32 = jnp.float32


def mat_mul(p, q):
    return (
        p[0] * q[0] + p[1] * q[2],
        p[0] * q[1] + p[1] * q[3],
        p[2] * q[0] + p[3] * q[2],
        p[2] * q[1] + p[3] * q[3],
    )


def mat_vec(p, v):
    return (p[0] * v[0] + p[1] * v[1], p[2] * v[0] + p[3] * v[1])


def mat_inv(p):
    inv = 1.0 / (p[0] * p[3] - p[1] * p[2])
    return (p[3] * inv, -p[1] * inv, -p[2] * inv, p[0] * inv)


def add(p, q):
    return tuple(x + y for x, y in zip(p, q))


def chunked(lo, hi, unroll, body, carry):
    whole = (hi - lo) // unroll

    def group(step, c):
        for u in range(unroll):
            c = body(lo + step * unroll + u, c)
        return c

    carry = lax.fori_loop(0, whole, group, carry)
    for i in range(lo + whole * unroll, hi):
        carry = body(i, carry)
    return carry


def y_forward(cot, diff, speed, upwind, codes, f_out, g_out, h_out, pack, low, left, right, rhs, first):
    rows_x, length = cot.shape[2], cot.shape[3]
    chunks = rows_x // LANES
    width = 2 * chunks
    boundary = lax.axis_index("yd") == 0
    for j in range(chunks):
        span = pl.ds(j * LANES, LANES)
        sp = speed[0, span, :]
        sm = sp * upwind[0, span, :].astype(F32)
        smt = sm.T
        snt = (sp - sm).T
        for c in range(2):
            slot = c * chunks + j
            df = diff[c, 0, span, :].T
            where = pl.ds(slot, length, stride=width)
            left[where, :] = smt + df
            right[where, :] = snt + df
            rhs[where, :] = cot[c, 0, span, :].T
            first[0, pl.ds(slot, 1), :] = snt[0:1, :]
            first[1, pl.ds(slot, 1), :] = df[0:1, :]
            first[2, pl.ds(slot, 1), :] = codes[0:1, span].astype(F32)

    def at(ref, i):
        return ref[pl.ds(pl.multiple_of(i * width, width), width), :]

    kind = first[2]
    edge = jnp.where(kind >= 0.5, first[0], 0.0) + jnp.where(jnp.abs(kind - 1.0) < 0.5, first[1], 0.0)
    r0 = jnp.where(boundary, edge, at(right, 0))
    right[pl.ds(0, width), :] = r0

    def step(i, carry):
        g, m, h, a_all, k_all, v_all = carry
        a = at(left, i + 1)
        r = at(right, i)
        rm = 1.0 + r * m
        rg = r * g
        inv = 1.0 / ((rm + a) + rg)
        m = rm * inv
        g = rg * inv
        h = (at(rhs, i) + r * h) * inv
        f = a * inv
        f_out[i] = f
        g_out[i] = g
        h_out[i] = h
        return (g, m, h, a_all * f, k_all + a_all * m, v_all + a_all * h)

    zero = jnp.zeros((width, LANES), F32)
    one = zero + 1.0
    g, m, h, a_all, k_all, v_all = chunked(0, length - 1, 8, step, (one, zero, zero, one, zero, zero))
    r = at(right, length - 1)
    a0 = at(left, 0)
    pack[0] = r * g
    pack[1] = 1.0 + r * m
    pack[2] = at(rhs, length - 1) + r * h
    pack[3] = a0 * a_all
    pack[4] = a0 * k_all
    pack[5] = a0 * v_all
    f_out[length - 1] = zero
    g_out[length - 1] = zero
    h_out[length - 1] = zero


def gather_kernel(axis, count, src, out, send_sem, recv_sem, own_sem):
    me = lax.axis_index(axis)
    barrier = pltpu.get_barrier_semaphore()
    for k in range(1, count):
        pl.semaphore_signal(
            barrier, inc=1, device_id={axis: lax.rem(me + k, count)}, device_id_type=pl.DeviceIdType.MESH
        )
    own = pltpu.make_async_copy(src, out.at[me], own_sem)
    own.start()
    pl.semaphore_wait(barrier, count - 1)
    copies = []
    for k in range(1, count):
        copy = pltpu.make_async_remote_copy(
            src_ref=src,
            dst_ref=out.at[me],
            send_sem=send_sem.at[k - 1],
            recv_sem=recv_sem.at[k - 1],
            device_id={axis: lax.rem(me + k, count)},
            device_id_type=pl.DeviceIdType.MESH,
        )
        copy.start()
        copies.append(copy)
    own.wait()
    for copy in copies:
        copy.wait()


def gather(axis, count, block, ident):
    return pl.pallas_call(
        functools.partial(gather_kernel, axis, count),
        out_shape=jax.ShapeDtypeStruct((count,) + block.shape, block.dtype),
        in_specs=[pl.BlockSpec(memory_space=pltpu.VMEM)],
        out_specs=pl.BlockSpec(memory_space=pltpu.VMEM),
        scratch_shapes=[
            pltpu.SemaphoreType.DMA((max(count - 1, 1),)),
            pltpu.SemaphoreType.DMA((max(count - 1, 1),)),
            pltpu.SemaphoreType.DMA,
        ],
        compiler_params=pltpu.CompilerParams(collective_id=ident, has_side_effects=True),
        name="gather_" + axis,
    )(block)


def middle(ny, packs, fy, gy, hy, diff, speed, upwind, coupling, codes,
           fx, gx, hx, chain, pack, q_all, lines, weights, edges):
    width = fy.shape[1]
    length = fy.shape[0]
    zero = jnp.zeros((width, LANES), F32)
    slack, h = zero + 1.0, zero
    factors = []
    for j in range(ny):
        lo, sg, v = packs[j, 0], packs[j, 1], packs[j, 2]
        up = zero
        if j + 1 < ny:
            up = packs[j + 1, 3]
            sg = sg + packs[j + 1, 4]
            v = v + packs[j + 1, 5]
        t = sg + lo * slack
        inv = 1.0 / (t + up)
        slack = t * inv
        h = (v + lo * h) * inv
        factors.append((up * inv, h))
    q = zero
    for j in reversed(range(ny)):
        f, h = factors[j]
        q = f * q + h
        q_all[j + 1] = q
    q_all[0] = zero
    me = lax.axis_index("yd")
    p = q_all[me]
    q = q_all[me + 1]

    def put(i, value):
        lines[pl.ds(pl.multiple_of(i * width, width), width), :] = value

    put(length - 1, q)

    def back(n, w):
        i = length - 2 - n
        w = fy[i] * w + (gy[i] * p + hy[i])
        put(i, w)
        return w

    chunked(0, length - 1, 8, back, q)
    rows_x = diff.shape[2]
    chunks = rows_x // LANES
    for c in range(2):
        for j in range(chunks):
            block = lines[pl.ds(c * chunks + j, length, stride=width), :]
            weights[c, pl.ds(j * LANES, LANES), :] = block.T

    depth = rows_x // SUB
    at_start = lax.axis_index("xg") == 0

    def rows(k):
        return pl.ds(k, SUB, stride=depth)

    def lefts(k):
        sm = speed[0, rows(k), :] * upwind[0, rows(k), :].astype(F32)
        return (sm + diff[0, 0, rows(k), :], sm + diff[1, 0, rows(k), :])

    def rights(k):
        sp = speed[0, rows(k), :]
        sn = sp - sp * upwind[0, rows(k), :].astype(F32)
        return (sn, diff[0, 0, rows(k), :], diff[1, 0, rows(k), :])

    def sigma(k):
        return (
            1.0 + 0.5 * coupling[0, 0, rows(k), :],
            0.5 * coupling[2, 0, rows(k), :],
            0.5 * coupling[1, 0, rows(k), :],
            1.0 + 0.5 * coupling[3, 0, rows(k), :],
        )

    def step(k, carry, r):
        g, m, h, a_all, k_all, v_all = carry
        a = lefts(k + 1)
        sg = sigma(k)
        rm = (sg[0] + r[0] * m[0], sg[1] + r[0] * m[1], sg[2] + r[1] * m[2], sg[3] + r[1] * m[3])
        rg = (r[0] * g[0], r[0] * g[1], r[1] * g[2], r[1] * g[3])
        d = (rm[0] + a[0] + rg[0], rm[1] + rg[1], rm[2] + rg[2], rm[3] + a[1] + rg[3])
        inv = mat_inv(d)
        m = mat_mul(inv, rm)
        g = mat_mul(inv, rg)
        f = (inv[0] * a[0], inv[1] * a[1], inv[2] * a[0], inv[3] * a[1])
        h = mat_vec(inv, tuple(weights[c, rows(k), :] + r[c] * h[c] for c in range(2)))
        for e in range(4):
            fx[k, e] = f[e]
            gx[k, e] = g[e]
        for c in range(2):
            hx[k, c] = h[c]
        return (
            g, m, h, mat_mul(a_all, f), add(k_all, mat_mul(a_all, m)), add(v_all, mat_vec(a_all, h)),
        )

    zero = jnp.zeros((SUB, LANES), F32)
    one = zero + 1.0
    unit = (one, zero, zero, one)
    none = (zero,) * 4
    kind = codes[0:1, :]
    top = (lax.broadcasted_iota(jnp.int32, (SUB, LANES), 0) == 0) & at_start
    sn, d0, d1 = rights(0)
    vented = (kind >= 1).astype(F32)
    opened = (kind == 1).astype(F32)
    r_first = tuple(jnp.where(top, vented * sn + opened * d, sn + d) for d in (d0, d1))
    carry = step(0, (unit, none, (zero, zero), unit, none, (zero, zero)), r_first)

    def inner(k, c):
        sn, d0, d1 = rights(k)
        return step(k, c, (sn + d0, sn + d1))

    g, m, h, a_all, k_all, v_all = chunked(1, depth - 1, 2, inner, carry)
    sn, d0, d1 = rights(depth - 1)
    r = (sn + d0, sn + d1)
    sg = sigma(depth - 1)
    rr = (r[0], r[0], r[1], r[1])
    a0 = lefts(0)
    aa = (a0[0], a0[0], a0[1], a0[1])
    for e in range(4):
        edges[e] = rr[e] * g[e]
        edges[4 + e] = sg[e] + rr[e] * m[e]
        edges[10 + e] = aa[e] * a_all[e]
        edges[14 + e] = aa[e] * k_all[e]
    for c in range(2):
        edges[8 + c] = weights[c, rows(depth - 1), :] + r[c] * h[c]
        edges[18 + c] = a0[c] * v_all[c]

    def edge(first, n, s):
        return tuple(edges[first + e, pl.ds(s, 1), :] for e in range(n))

    zrow = jnp.zeros((1, LANES), F32)
    orow = zrow + 1.0
    g, m, h = (orow, zrow, zrow, orow), (zrow,) * 4, (zrow, zrow)
    a_all, k_all, v_all = edge(10, 4, 0), edge(14, 4, 0), edge(18, 2, 0)
    for s in range(SUB - 1):
        lo, up = edge(0, 4, s), edge(10, 4, s + 1)
        sg = add(edge(4, 4, s), edge(14, 4, s + 1))
        v = add(edge(8, 2, s), edge(18, 2, s + 1))
        rm = add(sg, mat_mul(lo, m))
        rg = mat_mul(lo, g)
        inv = mat_inv(add(add(rm, up), rg))
        m, g, f = mat_mul(inv, rm), mat_mul(inv, rg), mat_mul(inv, up)
        h = mat_vec(inv, add(v, mat_vec(lo, h)))
        for e in range(4):
            chain[s, pl.ds(e, 1), :] = f[e]
            chain[s, pl.ds(4 + e, 1), :] = g[e]
        for c in range(2):
            chain[s, pl.ds(8 + c, 1), :] = h[c]
        k_all = add(k_all, mat_mul(a_all, m))
        v_all = add(v_all, mat_vec(a_all, h))
        a_all = mat_mul(a_all, f)
    last = SUB - 1
    lo = edge(0, 4, last)
    sent = (
        mat_mul(lo, g)
        + add(edge(4, 4, last), mat_mul(lo, m))
        + add(edge(8, 2, last), mat_vec(lo, h))
        + a_all
        + k_all
        + v_all
    )
    for e, row in enumerate(sent):
        pack[pl.ds(e, 1), :] = row
    for e in range(len(sent), pack.shape[0]):
        pack[pl.ds(e, 1), :] = zrow


def x_backward(nx, packs, chain, fx, gx, hx, out, q_all, before, own):
    def row(j, first, n):
        return tuple(packs[j, pl.ds(first + e, 1), :] for e in range(n))

    zrow = jnp.zeros((1, LANES), F32)
    orow = zrow + 1.0
    slack, h = (orow, zrow, zrow, orow), (zrow, zrow)
    factors = []
    for j in range(nx):
        lo, sg, v = row(j, 0, 4), row(j, 4, 4), row(j, 8, 2)
        up = (zrow,) * 4
        if j + 1 < nx:
            up = row(j + 1, 10, 4)
            sg = add(sg, row(j + 1, 14, 4))
            v = add(v, row(j + 1, 18, 2))
        t = add(sg, mat_mul(lo, slack))
        inv = mat_inv(add(t, up))
        slack = mat_mul(inv, t)
        h = mat_vec(inv, add(v, mat_vec(lo, h)))
        factors.append((mat_mul(inv, up), h))
    q = (zrow, zrow)
    for c in range(2):
        q_all[0, pl.ds(c, 1), :] = zrow
    for j in reversed(range(nx)):
        f, h = factors[j]
        q = add(mat_vec(f, q), h)
        for c in range(2):
            q_all[j + 1, pl.ds(c, 1), :] = q[c]
    me = lax.axis_index("xg")
    p = tuple(q_all[me, pl.ds(c, 1), :] for c in range(2))
    q = tuple(q_all[me + 1, pl.ds(c, 1), :] for c in range(2))
    for c in range(2):
        own[c, pl.ds(SUB - 1, 1), :] = q[c]
        before[c, pl.ds(0, 1), :] = p[c]
    for s in reversed(range(SUB - 1)):
        f = tuple(chain[s, pl.ds(e, 1), :] for e in range(4))
        g = tuple(chain[s, pl.ds(4 + e, 1), :] for e in range(4))
        h = tuple(chain[s, pl.ds(8 + c, 1), :] for c in range(2))
        q = add(mat_vec(f, q), add(mat_vec(g, p), h))
        for c in range(2):
            own[c, pl.ds(s, 1), :] = q[c]
            before[c, pl.ds(s + 1, 1), :] = q[c]
    depth = out.shape[2] // SUB
    prev = (before[0], before[1])
    x = (own[0], own[1])

    def put(k, x):
        for c in range(2):
            out[c, 0, pl.ds(k, SUB, stride=depth), :] = x[c]

    put(depth - 1, x)

    def back(n, x):
        k = depth - 2 - n
        f = tuple(fx[k, e] for e in range(4))
        g = tuple(gx[k, e] for e in range(4))
        base = add(mat_vec(g, prev), (hx[k, 0], hx[k, 1]))
        x = add(mat_vec(f, x), base)
        put(k, x)
        return x

    chunked(0, depth - 1, 8, back, x)


def call(body, outs, scratch, args, name):
    whole = pl.BlockSpec(memory_space=pltpu.VMEM)
    return pl.pallas_call(
        body,
        out_shape=[jax.ShapeDtypeStruct(s, F32) for s in outs],
        in_specs=[whole] * len(args),
        out_specs=[whole] * len(outs),
        scratch_shapes=[pltpu.VMEM(s, F32) for s in scratch],
        compiler_params=pltpu.CompilerParams(vmem_limit_bytes=40 * 1024 * 1024),
        name=name,
    )(*args)


def per_device(ny, nx, cotangent, x_diffusivity, x_speed, x_upwind, y_diffusivity, y_speed, y_upwind,
               coupling, x_codes, y_codes):
    rows_x, length = cotangent.shape[2], cotangent.shape[3]
    width = 2 * rows_x // LANES
    depth = rows_x // SUB
    tall = (length * width, LANES)
    fy, gy, hy, pack = call(
        y_forward,
        [(length, width, LANES)] * 3 + [(6, width, LANES)],
        [(8, LANES), tall, tall, tall, (3, width, LANES)],
        [cotangent, y_diffusivity, y_speed, y_upwind, y_codes],
        "y_forward",
    )
    packs = gather("yd", ny, pack, 1)
    fx, gx, hx, chain, pack = call(
        functools.partial(middle, ny),
        [(depth, 4, SUB, LANES), (depth, 4, SUB, LANES), (depth, 2, SUB, LANES),
         (SUB, 16, LANES), (24, LANES)],
        [(ny + 1, width, LANES), tall, (2, rows_x, LANES), (20, SUB, LANES)],
        [packs, fy, gy, hy, x_diffusivity, x_speed, x_upwind, coupling, x_codes],
        "middle",
    )
    packs = gather("xg", nx, pack, 2)
    (out,) = call(
        functools.partial(x_backward, nx),
        [cotangent.shape],
        [(nx + 1, SUB, LANES), (2, SUB, LANES), (2, SUB, LANES)],
        [packs, chain, fx, gx, hx],
        "x_backward",
    )
    return out


def solution(mesh):
    body = functools.partial(per_device, mesh.shape["yd"], mesh.shape["xg"])
    return jax.shard_map(
        body,
        mesh=mesh,
        in_specs=(
            P(None, None, "xg", "yd"),
            P(None, None, "xg", "yd"),
            P(None, "xg", "yd"),
            P(None, "xg", "yd"),
            P(None, None, "xg", "yd"),
            P(None, "xg", "yd"),
            P(None, "xg", "yd"),
            P(None, None, "xg", "yd"),
            P(None, "yd"),
            P(None, "xg"),
        ),
        out_specs=P(None, None, "xg", "yd"),
        check_vma=False,
    )
```

```python
import functools

import jax
import jax.numpy as jnp
from jax import lax
from jax.experimental import pallas as pl
from jax.experimental.pallas import tpu as pltpu
from jax.sharding import PartitionSpec as P

LANES = 128
SUB = 8
F32 = jnp.float32


def mat_mul(p, q):
    return (
        p[0] * q[0] + p[1] * q[2],
        p[0] * q[1] + p[1] * q[3],
        p[2] * q[0] + p[3] * q[2],
        p[2] * q[1] + p[3] * q[3],
    )


def mat_vec(p, v):
    return (p[0] * v[0] + p[1] * v[1], p[2] * v[0] + p[3] * v[1])


def mat_inv(p):
    inv = 1.0 / (p[0] * p[3] - p[1] * p[2])
    return (p[3] * inv, -p[1] * inv, -p[2] * inv, p[0] * inv)


def add(p, q):
    return tuple(x + y for x, y in zip(p, q))


def chunked(lo, hi, unroll, body, carry):
    whole = (hi - lo) // unroll

    def group(step, c):
        for u in range(unroll):
            c = body(lo + step * unroll + u, c)
        return c

    carry = lax.fori_loop(0, whole, group, carry)
    for i in range(lo + whole * unroll, hi):
        carry = body(i, carry)
    return carry


def y_forward(cot, diff, speed, upwind, codes, f_out, g_out, h_out, pack, left, right, rhs, first):
    rows_x, length = cot.shape[2], cot.shape[3]
    chunks = rows_x // LANES
    width = 2 * chunks
    boundary = lax.axis_index("yd") == 0
    for j in range(chunks):
        span = pl.ds(j * LANES, LANES)
        sp = speed[0, span, :]
        sm = sp * upwind[0, span, :].astype(F32)
        smt = sm.T
        snt = (sp - sm).T
        for c in range(2):
            slot = c * chunks + j
            df = diff[c, 0, span, :].T
            where = pl.ds(slot, length, stride=width)
            left[where, :] = smt + df
            right[where, :] = snt + df
            rhs[where, :] = cot[c, 0, span, :].T
            first[0, pl.ds(slot, 1), :] = snt[0:1, :]
            first[1, pl.ds(slot, 1), :] = df[0:1, :]
            first[2, pl.ds(slot, 1), :] = codes[0:1, span].astype(F32)

    def at(ref, i):
        return ref[pl.ds(pl.multiple_of(i * width, width), width), :]

    kind = first[2]
    edge = jnp.where(kind >= 0.5, first[0], 0.0) + jnp.where(jnp.abs(kind - 1.0) < 0.5, first[1], 0.0)
    r0 = jnp.where(boundary, edge, at(right, 0))
    right[pl.ds(0, width), :] = r0

    def step(i, carry):
        g, m, h, a_all, k_all, v_all = carry
        a = at(left, i + 1)
        r = at(right, i)
        rm = 1.0 + r * m
        rg = r * g
        inv = 1.0 / ((rm + a) + rg)
        m = rm * inv
        g = rg * inv
        h = (at(rhs, i) + r * h) * inv
        f = a * inv
        f_out[i] = f
        g_out[i] = g
        h_out[i] = h
        return (g, m, h, a_all * f, k_all + a_all * m, v_all + a_all * h)

    zero = jnp.zeros((width, LANES), F32)
    one = zero + 1.0
    g, m, h, a_all, k_all, v_all = chunked(0, length - 1, 8, step, (one, zero, zero, one, zero, zero))
    r = at(right, length - 1)
    a0 = at(left, 0)
    pack[0] = r * g
    pack[1] = 1.0 + r * m
    pack[2] = at(rhs, length - 1) + r * h
    pack[3] = a0 * a_all
    pack[4] = a0 * k_all
    pack[5] = a0 * v_all


def y_interfaces(ny, packs, q_all, width):
    zero = jnp.zeros((width, LANES), F32)
    slack, h = zero + 1.0, zero
    factors = []
    for j in range(ny):
        lo, sg, v = packs[j, 0], packs[j, 1], packs[j, 2]
        up = zero
        if j + 1 < ny:
            up = packs[j + 1, 3]
            sg = sg + packs[j + 1, 4]
            v = v + packs[j + 1, 5]
        t = sg + lo * slack
        inv = 1.0 / (t + up)
        slack = t * inv
        h = (v + lo * h) * inv
        factors.append((up * inv, h))
    q = zero
    for j in reversed(range(ny)):
        f, h = factors[j]
        q = f * q + h
        q_all[j + 1] = q
    q_all[0] = zero
    me = lax.axis_index("yd")
    return q_all[me], q_all[me + 1]


def y_backward(p, q, fy, gy, hy, lines, weights):
    length, width = fy.shape[0], fy.shape[1]

    def put(i, value):
        lines[pl.ds(pl.multiple_of(i * width, width), width), :] = value

    put(length - 1, q)

    def back(n, w):
        i = length - 2 - n
        w = fy[i] * w + (gy[i] * p + hy[i])
        put(i, w)
        return w

    chunked(0, length - 1, 8, back, q)
    chunks = width // 2
    for c in range(2):
        for j in range(chunks):
            block = lines[pl.ds(c * chunks + j, length, stride=width), :]
            weights[c, pl.ds(j * LANES, LANES), :] = block.T


def x_coefficients(diff, speed, upwind, coupling, codes, fx, gx, ix, nx_, ax, edges):
    depth = diff.shape[2] // SUB
    at_start = lax.axis_index("xg") == 0

    def rows(k):
        return pl.ds(k, SUB, stride=depth)

    def lefts(k):
        sm = speed[0, rows(k), :] * upwind[0, rows(k), :].astype(F32)
        return (sm + diff[0, 0, rows(k), :], sm + diff[1, 0, rows(k), :])

    def rights(k):
        sp = speed[0, rows(k), :]
        sn = sp - sp * upwind[0, rows(k), :].astype(F32)
        return (sn, diff[0, 0, rows(k), :], diff[1, 0, rows(k), :])

    def sigma(k):
        return (
            1.0 + 0.5 * coupling[0, 0, rows(k), :],
            0.5 * coupling[2, 0, rows(k), :],
            0.5 * coupling[1, 0, rows(k), :],
            1.0 + 0.5 * coupling[3, 0, rows(k), :],
        )

    def step(k, carry, r):
        g, m, a_all, k_all = carry
        a = lefts(k + 1)
        sg = sigma(k)
        rm = (sg[0] + r[0] * m[0], sg[1] + r[0] * m[1], sg[2] + r[1] * m[2], sg[3] + r[1] * m[3])
        rg = (r[0] * g[0], r[0] * g[1], r[1] * g[2], r[1] * g[3])
        d = (rm[0] + a[0] + rg[0], rm[1] + rg[1], rm[2] + rg[2], rm[3] + a[1] + rg[3])
        inv = mat_inv(d)
        m = mat_mul(inv, rm)
        g = mat_mul(inv, rg)
        f = (inv[0] * a[0], inv[1] * a[1], inv[2] * a[0], inv[3] * a[1])
        n = (inv[0] * r[0], inv[1] * r[1], inv[2] * r[0], inv[3] * r[1])
        for e in range(4):
            fx[k, e] = f[e]
            gx[k, e] = g[e]
            ix[k, e] = inv[e]
            nx_[k, e] = n[e]
            ax[k, e] = a_all[e]
        return (g, m, mat_mul(a_all, f), add(k_all, mat_mul(a_all, m)))

    zero = jnp.zeros((SUB, LANES), F32)
    one = zero + 1.0
    unit = (one, zero, zero, one)
    none = (zero,) * 4
    kind = codes[0:1, :]
    top = (lax.broadcasted_iota(jnp.int32, (SUB, LANES), 0) == 0) & at_start
    sn, d0, d1 = rights(0)
    vented = (kind >= 1).astype(F32)
    opened = (kind == 1).astype(F32)
    r_first = tuple(jnp.where(top, vented * sn + opened * d, sn + d) for d in (d0, d1))
    carry = step(0, (unit, none, unit, none), r_first)

    def inner(k, c):
        sn, d0, d1 = rights(k)
        return step(k, c, (sn + d0, sn + d1))

    g, m, a_all, k_all = chunked(1, depth - 1, 2, inner, carry)
    sn, d0, d1 = rights(depth - 1)
    r = (sn + d0, sn + d1)
    sg = sigma(depth - 1)
    rr = (r[0], r[0], r[1], r[1])
    a0 = lefts(0)
    aa = (a0[0], a0[0], a0[1], a0[1])
    for e in range(4):
        edges[e] = rr[e] * g[e]
        edges[4 + e] = sg[e] + rr[e] * m[e]
        edges[8 + e] = aa[e] * a_all[e]
        edges[12 + e] = aa[e] * k_all[e]
    for c in range(2):
        edges[20 + c] = a0[c]
        edges[22 + c] = r[c]


def edge_rows(edges, first, n, s):
    return tuple(edges[first + e, pl.ds(s, 1), :] for e in range(n))


def x_chain_coefficients(edges, chain, pack, me):
    zrow = jnp.zeros((1, LANES), F32)
    orow = zrow + 1.0
    g, m = (orow, zrow, zrow, orow), (zrow,) * 4
    a_all, k_all = edge_rows(edges, 8, 4, 0), edge_rows(edges, 12, 4, 0)
    for s in range(SUB - 1):
        lo, up = edge_rows(edges, 0, 4, s), edge_rows(edges, 8, 4, s + 1)
        sg = add(edge_rows(edges, 4, 4, s), edge_rows(edges, 12, 4, s + 1))
        rm = add(sg, mat_mul(lo, m))
        rg = mat_mul(lo, g)
        inv = mat_inv(add(add(rm, up), rg))
        m, g, f = mat_mul(inv, rm), mat_mul(inv, rg), mat_mul(inv, up)
        for e in range(4):
            chain[s, pl.ds(e, 1), :] = f[e]
            chain[s, pl.ds(4 + e, 1), :] = g[e]
            chain[s, pl.ds(8 + e, 1), :] = inv[e]
            chain[s, pl.ds(12 + e, 1), :] = a_all[e]
        k_all = add(k_all, mat_mul(a_all, m))
        a_all = mat_mul(a_all, f)
    lo = edge_rows(edges, 0, 4, SUB - 1)
    sent = mat_mul(lo, g) + add(edge_rows(edges, 4, 4, SUB - 1), mat_mul(lo, m)) + a_all + k_all
    for e, row in enumerate(sent):
        pack[me, pl.ds(e, 1), :] = row


def x_values(weights, ix, nx_, ax, hx, edges):
    depth = weights.shape[1] // SUB

    def step(k, carry):
        h, v_all = carry
        w = tuple(weights[c, pl.ds(k, SUB, stride=depth), :] for c in range(2))
        base = mat_vec(tuple(ix[k, e] for e in range(4)), w)
        n = tuple(nx_[k, e] for e in range(4))
        a_all = tuple(ax[k, e] for e in range(4))
        h = ((base[0] + n[0] * h[0]) + n[1] * h[1], (base[1] + n[2] * h[0]) + n[3] * h[1])
        for c in range(2):
            hx[k, c] = h[c]
        return h, add(v_all, mat_vec(a_all, h))

    zero = jnp.zeros((SUB, LANES), F32)
    h, v_all = chunked(0, depth - 1, 7, step, ((zero, zero), (zero, zero)))
    for c in range(2):
        edges[16 + c] = weights[c, pl.ds(depth - 1, SUB, stride=depth), :] + edges[22 + c] * h[c]
        edges[18 + c] = edges[20 + c] * v_all[c]


def x_chain_values(edges, chain, sums, pack, me):
    zrow = jnp.zeros((1, LANES), F32)
    h = (zrow, zrow)
    v_all = edge_rows(edges, 18, 2, 0)
    for s in range(SUB - 1):
        lo = edge_rows(edges, 0, 4, s)
        v = add(edge_rows(edges, 16, 2, s), edge_rows(edges, 18, 2, s + 1))
        inv = tuple(chain[s, pl.ds(8 + e, 1), :] for e in range(4))
        a_all = tuple(chain[s, pl.ds(12 + e, 1), :] for e in range(4))
        h = mat_vec(inv, add(v, mat_vec(lo, h)))
        for c in range(2):
            sums[s, pl.ds(c, 1), :] = h[c]
        v_all = add(v_all, mat_vec(a_all, h))
    lo = edge_rows(edges, 0, 4, SUB - 1)
    sent = add(edge_rows(edges, 16, 2, SUB - 1), mat_vec(lo, h)) + v_all
    for e in range(SUB):
        pack[me, pl.ds(e, 1), :] = sent[e] if e < len(sent) else zrow


def x_backward(nx, coefs, values, chain, sums, fx, gx, hx, out, q_all, before, own):
    def row(ref, j, first, n):
        return tuple(ref[j, pl.ds(first + e, 1), :] for e in range(n))

    zrow = jnp.zeros((1, LANES), F32)
    orow = zrow + 1.0
    slack, h = (orow, zrow, zrow, orow), (zrow, zrow)
    factors = []
    for j in range(nx):
        lo, sg, v = row(coefs, j, 0, 4), row(coefs, j, 4, 4), row(values, j, 0, 2)
        up = (zrow,) * 4
        if j + 1 < nx:
            up = row(coefs, j + 1, 8, 4)
            sg = add(sg, row(coefs, j + 1, 12, 4))
            v = add(v, row(values, j + 1, 2, 2))
        t = add(sg, mat_mul(lo, slack))
        inv = mat_inv(add(t, up))
        slack = mat_mul(inv, t)
        h = mat_vec(inv, add(v, mat_vec(lo, h)))
        factors.append((mat_mul(inv, up), h))
    q = (zrow, zrow)
    for c in range(2):
        q_all[0, pl.ds(c, 1), :] = zrow
    for j in reversed(range(nx)):
        f, h = factors[j]
        q = add(mat_vec(f, q), h)
        for c in range(2):
            q_all[j + 1, pl.ds(c, 1), :] = q[c]
    me = lax.axis_index("xg")
    p = tuple(q_all[me, pl.ds(c, 1), :] for c in range(2))
    q = tuple(q_all[me + 1, pl.ds(c, 1), :] for c in range(2))
    for c in range(2):
        own[c, pl.ds(SUB - 1, 1), :] = q[c]
        before[c, pl.ds(0, 1), :] = p[c]
    for s in reversed(range(SUB - 1)):
        f = tuple(chain[s, pl.ds(e, 1), :] for e in range(4))
        g = tuple(chain[s, pl.ds(4 + e, 1), :] for e in range(4))
        h = tuple(sums[s, pl.ds(c, 1), :] for c in range(2))
        q = add(mat_vec(f, q), add(mat_vec(g, p), h))
        for c in range(2):
            own[c, pl.ds(s, 1), :] = q[c]
            before[c, pl.ds(s + 1, 1), :] = q[c]
    depth = out.shape[1] // SUB
    prev = (before[0], before[1])
    x = (own[0], own[1])

    def put(k, x):
        for c in range(2):
            out[c, pl.ds(k, SUB, stride=depth), :] = x[c]

    put(depth - 1, x)

    def back(n, x):
        k = depth - 2 - n
        f = tuple(fx[k, e] for e in range(4))
        g = tuple(gx[k, e] for e in range(4))
        base = add(mat_vec(g, prev), (hx[k, 0], hx[k, 1]))
        x = add(mat_vec(f, x), base)
        put(k, x)
        return x

    chunked(0, depth - 1, 8, back, x)


def sends(axis, count, ref, send_sem, recv_sem):
    me = lax.axis_index(axis)
    return [
        pltpu.make_async_remote_copy(
            src_ref=ref.at[me],
            dst_ref=ref.at[me],
            send_sem=send_sem.at[k - 1],
            recv_sem=recv_sem.at[k - 1],
            device_id={axis: lax.rem(me + k, count)},
            device_id_type=pl.DeviceIdType.MESH,
        )
        for k in range(1, count)
    ]


def kernel(ny, nx, *refs):
    sources, out_hbm = refs[:10], refs[10]
    held = refs[11:21]
    (fy, gy, hy, left, right, rhs, first, y_packs, q_y, weights, fx, gx, ix, nx_, ax, hx, edges,
     chain, sums, x_coefs, x_vals, q_x, before, own, out,
     in_sem, y_send, y_recv, c_send, c_recv, v_send, v_recv, out_sem) = refs[21:]
    cot, x_diff, x_speed, x_up, y_diff, y_speed, y_up, coupling, x_codes, y_codes = held
    loads = [pltpu.make_async_copy(s, d, in_sem.at[i]) for i, (s, d) in enumerate(zip(sources, held))]
    y_order, x_order = (5, 6, 4, 0, 9), (2, 3, 1, 7, 8)
    for i in y_order + x_order:
        loads[i].start()
    barrier = pltpu.get_barrier_semaphore()
    for axis, count in (("yd", ny), ("xg", nx)):
        for k in range(1, count):
            peer = lax.rem(lax.axis_index(axis) + k, count)
            pl.semaphore_signal(barrier, inc=1, device_id={axis: peer}, device_id_type=pl.DeviceIdType.MESH)
    for i in y_order:
        loads[i].wait()
    me_y, me_x = lax.axis_index("yd"), lax.axis_index("xg")
    y_forward(cot, y_diff, y_speed, y_up, y_codes, fy, gy, hy, y_packs.at[me_y], left, right, rhs, first)
    pl.semaphore_wait(barrier, ny + nx - 2)
    y_copies = sends("yd", ny, y_packs, y_send, y_recv)
    for copy in y_copies:
        copy.start()
    for i in x_order:
        loads[i].wait()
    x_coefficients(x_diff, x_speed, x_up, coupling, x_codes, fx, gx, ix, nx_, ax, edges)
    x_chain_coefficients(edges, chain, x_coefs, me_x)
    c_copies = sends("xg", nx, x_coefs, c_send, c_recv)
    for copy in c_copies:
        copy.start()
    for copy in y_copies:
        copy.wait()
    p, q = y_interfaces(ny, y_packs, q_y, fy.shape[1])
    y_backward(p, q, fy, gy, hy, left, weights)
    x_values(weights, ix, nx_, ax, hx, edges)
    x_chain_values(edges, chain, sums, x_vals, me_x)
    v_copies = sends("xg", nx, x_vals, v_send, v_recv)
    for copy in v_copies:
        copy.start()
    for copy in c_copies:
        copy.wait()
    for copy in v_copies:
        copy.wait()
    x_backward(nx, x_coefs, x_vals, chain, sums, fx, gx, hx, out, q_x, before, own)
    stores = [pltpu.make_async_copy(out.at[c], out_hbm.at[c, 0], out_sem.at[c]) for c in range(2)]
    for copy in stores:
        copy.start()
    for copy in stores:
        copy.wait()


def per_device(ny, nx, *args):
    rows_x, length = args[0].shape[2], args[0].shape[3]
    width = 2 * rows_x // LANES
    depth = rows_x // SUB
    tall = (length * width, LANES)
    deep = (length, width, LANES)
    quad = (depth, 4, SUB, LANES)
    shapes = [
        deep, deep, deep, tall, tall, tall, (3, width, LANES), (ny, 6, width, LANES), (ny + 1, width, LANES),
        (2, rows_x, LANES), quad, quad, quad, quad, quad, (depth, 2, SUB, LANES), (24, SUB, LANES),
        (SUB, 16, LANES), (SUB, SUB, LANES), (nx, 16, LANES), (nx, SUB, LANES), (nx + 1, SUB, LANES),
        (2, SUB, LANES), (2, SUB, LANES), (2, rows_x, LANES),
    ]
    dma = pltpu.SemaphoreType.DMA
    return pl.pallas_call(
        functools.partial(kernel, ny, nx),
        out_shape=jax.ShapeDtypeStruct(args[0].shape, F32),
        in_specs=[pl.BlockSpec(memory_space=pl.ANY)] * len(args),
        out_specs=pl.BlockSpec(memory_space=pl.ANY),
        scratch_shapes=[pltpu.VMEM(a.shape, a.dtype) for a in args]
        + [pltpu.VMEM(s, F32) for s in shapes]
        + [dma((len(args),)), dma((ny - 1,)), dma((ny - 1,)), dma((nx - 1,)), dma((nx - 1,)),
           dma((nx - 1,)), dma((nx - 1,)), dma((2,))],
        compiler_params=pltpu.CompilerParams(
            collective_id=0, has_side_effects=True, vmem_limit_bytes=56 * 1024 * 1024
        ),
        name="adjoint_step",
    )(*args)


def solution(mesh):
    body = functools.partial(per_device, mesh.shape["yd"], mesh.shape["xg"])
    return jax.shard_map(
        body,
        mesh=mesh,
        in_specs=(
            P(None, None, "xg", "yd"),
            P(None, None, "xg", "yd"),
            P(None, "xg", "yd"),
            P(None, "xg", "yd"),
            P(None, None, "xg", "yd"),
            P(None, "xg", "yd"),
            P(None, "xg", "yd"),
            P(None, None, "xg", "yd"),
            P(None, "yd"),
            P(None, "xg"),
        ),
        out_specs=P(None, None, "xg", "yd"),
        check_vma=False,
    )
```

```python
import functools

import jax
import jax.numpy as jnp
from jax import lax
from jax.experimental import pallas as pl
from jax.experimental.pallas import tpu as pltpu
from jax.sharding import PartitionSpec as P

LANES = 128
SUB = 8
PARTS = 4
F32 = jnp.float32


def mat_mul(p, q):
    return (
        p[0] * q[0] + p[1] * q[2],
        p[0] * q[1] + p[1] * q[3],
        p[2] * q[0] + p[3] * q[2],
        p[2] * q[1] + p[3] * q[3],
    )


def mat_vec(p, v):
    return (p[0] * v[0] + p[1] * v[1], p[2] * v[0] + p[3] * v[1])


def mat_inv(p):
    inv = 1.0 / (p[0] * p[3] - p[1] * p[2])
    return (p[3] * inv, -p[1] * inv, -p[2] * inv, p[0] * inv)


def add(p, q):
    return tuple(x + y for x, y in zip(p, q))


def chunked(lo, hi, unroll, body, carry):
    whole = (hi - lo) // unroll

    def group(step, c):
        for u in range(unroll):
            c = body(lo + step * unroll + u, c)
        return c

    carry = lax.fori_loop(0, whole, group, carry)
    for i in range(lo + whole * unroll, hi):
        carry = body(i, carry)
    return carry


def y_forward(cot, diff, speed, upwind, codes, f_out, g_out, h_out, pack, left, right, rhs, first, joint):
    rows_x, length = cot.shape[2], cot.shape[3]
    chunks = rows_x // LANES
    width = 2 * chunks
    boundary = lax.axis_index("yd") == 0
    for j in range(chunks):
        span = pl.ds(j * LANES, LANES)
        sp = speed[0, span, :]
        sm = sp * upwind[0, span, :].astype(F32)
        smt = sm.T
        snt = (sp - sm).T
        for c in range(2):
            slot = c * chunks + j
            df = diff[c, 0, span, :].T
            where = pl.ds(slot, length, stride=width)
            left[where, :] = smt + df
            right[where, :] = snt + df
            rhs[where, :] = cot[c, 0, span, :].T
            first[0, pl.ds(slot, 1), :] = snt[0:1, :]
            first[1, pl.ds(slot, 1), :] = df[0:1, :]
            first[2, pl.ds(slot, 1), :] = codes[0:1, span].astype(F32)

    def at(ref, i):
        return ref[pl.ds(pl.multiple_of(i * width, width), width), :]

    kind = first[2]
    edge = jnp.where(kind >= 0.5, first[0], 0.0) + jnp.where(jnp.abs(kind - 1.0) < 0.5, first[1], 0.0)
    r0 = jnp.where(boundary, edge, at(right, 0))
    right[pl.ds(0, width), :] = r0

    def step(i, carry):
        g, m, h, a_all, k_all, v_all = carry
        a = at(left, i + 1)
        r = at(right, i)
        rm = 1.0 + r * m
        rg = r * g
        inv = 1.0 / ((rm + a) + rg)
        m = rm * inv
        g = rg * inv
        h = (at(rhs, i) + r * h) * inv
        f = a * inv
        f_out[i] = f
        g_out[i] = g
        h_out[i] = h
        return (g, m, h, a_all * f, k_all + a_all * m, v_all + a_all * h)

    zero = jnp.zeros((width, LANES), F32)
    one = zero + 1.0
    seg = length // PARTS

    def abreast(i, carries):
        return tuple(step(n * seg + i, c) for n, c in enumerate(carries))

    start = ((one, zero, zero, one, zero, zero),) * PARTS
    parts = []
    for n, (g, m, h, a_all, k_all, v_all) in enumerate(chunked(0, seg - 1, 4, abreast, start)):
        r = at(right, (n + 1) * seg - 1)
        a0 = at(left, n * seg)
        v = at(rhs, (n + 1) * seg - 1) + r * h
        parts.append((r * g, 1.0 + r * m, v, a0 * a_all, a0 * k_all, a0 * v_all))
    g, m, h = one, zero, zero
    a_all, k_all, v_all = parts[0][3:]
    for n in range(PARTS - 1):
        lo, sg, v = parts[n][:3]
        up, k_next, v_next = parts[n + 1][3:]
        rm = (sg + k_next) + lo * m
        rg = lo * g
        inv = 1.0 / ((rm + up) + rg)
        m = rm * inv
        g = rg * inv
        h = ((v + v_next) + lo * h) * inv
        f = up * inv
        joint[n, 0] = f
        joint[n, 1] = g
        joint[n, 2] = h
        k_all = k_all + a_all * m
        v_all = v_all + a_all * h
        a_all = a_all * f
    lo, sg, v = parts[-1][:3]
    for e, value in enumerate((lo * g, sg + lo * m, v + lo * h, a_all, k_all, v_all)):
        pack[e] = value


def y_interfaces(ny, packs, q_all, width):
    zero = jnp.zeros((width, LANES), F32)
    slack, h = zero + 1.0, zero
    factors = []
    for j in range(ny):
        lo, sg, v = packs[j, 0], packs[j, 1], packs[j, 2]
        up = zero
        if j + 1 < ny:
            up = packs[j + 1, 3]
            sg = sg + packs[j + 1, 4]
            v = v + packs[j + 1, 5]
        t = sg + lo * slack
        inv = 1.0 / (t + up)
        slack = t * inv
        h = (v + lo * h) * inv
        factors.append((up * inv, h))
    q = zero
    for j in reversed(range(ny)):
        f, h = factors[j]
        q = f * q + h
        q_all[j + 1] = q
    q_all[0] = zero
    me = lax.axis_index("yd")
    return q_all[me], q_all[me + 1]


def y_backward(p, q, fy, gy, hy, joint, lines, weights):
    length, width = fy.shape[0], fy.shape[1]

    def put(i, value):
        lines[pl.ds(pl.multiple_of(i * width, width), width), :] = value

    seg = length // PARTS
    ends = [q]
    for n in reversed(range(PARTS - 1)):
        ends.insert(0, joint[n, 0] * ends[0] + (joint[n, 1] * p + joint[n, 2]))
    starts = [p] + ends[:-1]
    for n in range(PARTS):
        put((n + 1) * seg - 1, ends[n])

    def back(k, ws):
        done = []
        for n, w in enumerate(ws):
            i = (n + 1) * seg - 2 - k
            w = fy[i] * w + (gy[i] * starts[n] + hy[i])
            put(i, w)
            done.append(w)
        return tuple(done)

    chunked(0, seg - 1, 4, back, tuple(ends))
    chunks = width // 2
    for c in range(2):
        for j in range(chunks):
            block = lines[pl.ds(c * chunks + j, length, stride=width), :]
            weights[c, pl.ds(j * LANES, LANES), :] = block.T


def x_coefficients(diff, speed, upwind, coupling, codes, fx, gx, ix, nx_, ax, halves, edges):
    depth = diff.shape[2] // SUB
    at_start = lax.axis_index("xg") == 0

    def rows(k):
        return pl.ds(k, SUB, stride=depth)

    def lefts(k):
        sm = speed[0, rows(k), :] * upwind[0, rows(k), :].astype(F32)
        return (sm + diff[0, 0, rows(k), :], sm + diff[1, 0, rows(k), :])

    def rights(k):
        sp = speed[0, rows(k), :]
        sn = sp - sp * upwind[0, rows(k), :].astype(F32)
        return (sn, diff[0, 0, rows(k), :], diff[1, 0, rows(k), :])

    def sigma(k):
        return (
            1.0 + 0.5 * coupling[0, 0, rows(k), :],
            0.5 * coupling[2, 0, rows(k), :],
            0.5 * coupling[1, 0, rows(k), :],
            1.0 + 0.5 * coupling[3, 0, rows(k), :],
        )

    def step(k, carry, r):
        g, m, a_all, k_all = carry
        a = lefts(k + 1)
        sg = sigma(k)
        rm = (sg[0] + r[0] * m[0], sg[1] + r[0] * m[1], sg[2] + r[1] * m[2], sg[3] + r[1] * m[3])
        rg = (r[0] * g[0], r[0] * g[1], r[1] * g[2], r[1] * g[3])
        d = (rm[0] + a[0] + rg[0], rm[1] + rg[1], rm[2] + rg[2], rm[3] + a[1] + rg[3])
        inv = mat_inv(d)
        m = mat_mul(inv, rm)
        g = mat_mul(inv, rg)
        f = (inv[0] * a[0], inv[1] * a[1], inv[2] * a[0], inv[3] * a[1])
        n = (inv[0] * r[0], inv[1] * r[1], inv[2] * r[0], inv[3] * r[1])
        for e in range(4):
            fx[k, e] = f[e]
            gx[k, e] = g[e]
            ix[k, e] = inv[e]
            nx_[k, e] = n[e]
            ax[k, e] = a_all[e]
        return (g, m, mat_mul(a_all, f), add(k_all, mat_mul(a_all, m)))

    zero = jnp.zeros((SUB, LANES), F32)
    one = zero + 1.0
    unit = (one, zero, zero, one)
    none = (zero,) * 4
    kind = codes[0:1, :]
    top = (lax.broadcasted_iota(jnp.int32, (SUB, LANES), 0) == 0) & at_start
    sn, d0, d1 = rights(0)
    vented = (kind >= 1).astype(F32)
    opened = (kind == 1).astype(F32)
    r_first = tuple(jnp.where(top, vented * sn + opened * d, sn + d) for d in (d0, d1))
    half = depth // 2

    def plain(k):
        sn, d0, d1 = rights(k)
        return (sn + d0, sn + d1)

    def abreast(k, cs):
        return (step(k, cs[0], plain(k)), step(half + k, cs[1], plain(half + k)))

    fresh = (unit, none, unit, none)
    pair = (step(0, fresh, r_first), step(half, fresh, plain(half)))
    pair = chunked(1, half - 1, 2, abreast, pair)
    ends = []
    for n, (g, m, a_all, k_all) in enumerate(pair):
        end = (n + 1) * half - 1
        r = plain(end)
        rr = (r[0], r[0], r[1], r[1])
        a0 = lefts(n * half)
        aa = (a0[0], a0[0], a0[1], a0[1])
        sg = sigma(end)
        for c in range(2):
            halves[20 + 4 * n + c] = a0[c]
            halves[22 + 4 * n + c] = r[c]
        ends.append((
            tuple(x * y for x, y in zip(rr, g)),
            tuple(z + x * y for x, y, z in zip(rr, m, sg)),
            tuple(x * y for x, y in zip(aa, a_all)),
            tuple(x * y for x, y in zip(aa, k_all)),
        ))
    (lo, sg, a_all, k_all), (lo_end, sg_end, up, k_next) = ends
    sg = add(sg, k_next)
    inv = mat_inv(add(add(sg, lo), up))
    m, g, f = mat_mul(inv, sg), mat_mul(inv, lo), mat_mul(inv, up)
    lo_sub = mat_mul(lo_end, g)
    sg_sub = add(sg_end, mat_mul(lo_end, m))
    k_sub = add(k_all, mat_mul(a_all, m))
    a_sub = mat_mul(a_all, f)
    for e in range(4):
        halves[e] = f[e]
        halves[4 + e] = g[e]
        halves[8 + e] = inv[e]
        halves[12 + e] = lo_end[e]
        halves[16 + e] = a_all[e]
        edges[e] = lo_sub[e]
        edges[4 + e] = sg_sub[e]
        edges[8 + e] = a_sub[e]
        edges[12 + e] = k_sub[e]


def edge_rows(edges, first, n, s):
    return tuple(edges[first + e, pl.ds(s, 1), :] for e in range(n))


def x_chain_coefficients(edges, chain, pack, me):
    zrow = jnp.zeros((1, LANES), F32)
    orow = zrow + 1.0
    g, m = (orow, zrow, zrow, orow), (zrow,) * 4
    a_all, k_all = edge_rows(edges, 8, 4, 0), edge_rows(edges, 12, 4, 0)
    for s in range(SUB - 1):
        lo, up = edge_rows(edges, 0, 4, s), edge_rows(edges, 8, 4, s + 1)
        sg = add(edge_rows(edges, 4, 4, s), edge_rows(edges, 12, 4, s + 1))
        rm = add(sg, mat_mul(lo, m))
        rg = mat_mul(lo, g)
        inv = mat_inv(add(add(rm, up), rg))
        m, g, f = mat_mul(inv, rm), mat_mul(inv, rg), mat_mul(inv, up)
        for e in range(4):
            chain[s, pl.ds(e, 1), :] = f[e]
            chain[s, pl.ds(4 + e, 1), :] = g[e]
            chain[s, pl.ds(8 + e, 1), :] = inv[e]
            chain[s, pl.ds(12 + e, 1), :] = a_all[e]
        k_all = add(k_all, mat_mul(a_all, m))
        a_all = mat_mul(a_all, f)
    lo = edge_rows(edges, 0, 4, SUB - 1)
    sent = mat_mul(lo, g) + add(edge_rows(edges, 4, 4, SUB - 1), mat_mul(lo, m)) + a_all + k_all
    for e, row in enumerate(sent):
        pack[me, pl.ds(e, 1), :] = row


def x_values(weights, ix, nx_, ax, hx, halves, edges):
    depth = weights.shape[1] // SUB
    half = depth // 2

    def at(k):
        return tuple(weights[c, pl.ds(k, SUB, stride=depth), :] for c in range(2))

    def quad(ref, k):
        return tuple(ref[k, e] for e in range(4))

    def held(first, n):
        return tuple(halves[first + e] for e in range(n))

    def step(k, carry):
        h, v_all = carry
        base = mat_vec(quad(ix, k), at(k))
        n = quad(nx_, k)
        h = ((base[0] + n[0] * h[0]) + n[1] * h[1], (base[1] + n[2] * h[0]) + n[3] * h[1])
        for c in range(2):
            hx[k, c] = h[c]
        return h, add(v_all, mat_vec(quad(ax, k), h))

    def abreast(k, cs):
        return (step(k, cs[0]), step(half + k, cs[1]))

    zero = jnp.zeros((SUB, LANES), F32)
    fresh = ((zero, zero), (zero, zero))
    ends = []
    for n, (h, v_all) in enumerate(chunked(0, half - 1, 4, abreast, (fresh, fresh))):
        a0, r = held(20 + 4 * n, 2), held(22 + 4 * n, 2)
        w = at((n + 1) * half - 1)
        ends.append((tuple(w[c] + r[c] * h[c] for c in range(2)), tuple(a0[c] * v_all[c] for c in range(2))))
    (v, v_all), (v_end, v_next) = ends
    h = mat_vec(held(8, 4), add(v, v_next))
    v_end = add(v_end, mat_vec(held(12, 4), h))
    v_all = add(v_all, mat_vec(held(16, 4), h))
    for c in range(2):
        halves[28 + c] = h[c]
        edges[16 + c] = v_end[c]
        edges[18 + c] = v_all[c]


def x_chain_values(edges, chain, sums, pack, me):
    zrow = jnp.zeros((1, LANES), F32)
    h = (zrow, zrow)
    v_all = edge_rows(edges, 18, 2, 0)
    for s in range(SUB - 1):
        lo = edge_rows(edges, 0, 4, s)
        v = add(edge_rows(edges, 16, 2, s), edge_rows(edges, 18, 2, s + 1))
        inv = tuple(chain[s, pl.ds(8 + e, 1), :] for e in range(4))
        a_all = tuple(chain[s, pl.ds(12 + e, 1), :] for e in range(4))
        h = mat_vec(inv, add(v, mat_vec(lo, h)))
        for c in range(2):
            sums[s, pl.ds(c, 1), :] = h[c]
        v_all = add(v_all, mat_vec(a_all, h))
    lo = edge_rows(edges, 0, 4, SUB - 1)
    sent = add(edge_rows(edges, 16, 2, SUB - 1), mat_vec(lo, h)) + v_all
    for e in range(SUB):
        pack[me, pl.ds(e, 1), :] = sent[e] if e < len(sent) else zrow


def x_backward(nx, coefs, values, chain, sums, halves, fx, gx, hx, out, q_all, before, own):
    def row(ref, j, first, n):
        return tuple(ref[j, pl.ds(first + e, 1), :] for e in range(n))

    zrow = jnp.zeros((1, LANES), F32)
    orow = zrow + 1.0
    slack, h = (orow, zrow, zrow, orow), (zrow, zrow)
    factors = []
    for j in range(nx):
        lo, sg, v = row(coefs, j, 0, 4), row(coefs, j, 4, 4), row(values, j, 0, 2)
        up = (zrow,) * 4
        if j + 1 < nx:
            up = row(coefs, j + 1, 8, 4)
            sg = add(sg, row(coefs, j + 1, 12, 4))
            v = add(v, row(values, j + 1, 2, 2))
        t = add(sg, mat_mul(lo, slack))
        inv = mat_inv(add(t, up))
        slack = mat_mul(inv, t)
        h = mat_vec(inv, add(v, mat_vec(lo, h)))
        factors.append((mat_mul(inv, up), h))
    q = (zrow, zrow)
    for c in range(2):
        q_all[0, pl.ds(c, 1), :] = zrow
    for j in reversed(range(nx)):
        f, h = factors[j]
        q = add(mat_vec(f, q), h)
        for c in range(2):
            q_all[j + 1, pl.ds(c, 1), :] = q[c]
    me = lax.axis_index("xg")
    p = tuple(q_all[me, pl.ds(c, 1), :] for c in range(2))
    q = tuple(q_all[me + 1, pl.ds(c, 1), :] for c in range(2))
    for c in range(2):
        own[c, pl.ds(SUB - 1, 1), :] = q[c]
        before[c, pl.ds(0, 1), :] = p[c]
    for s in reversed(range(SUB - 1)):
        f = tuple(chain[s, pl.ds(e, 1), :] for e in range(4))
        g = tuple(chain[s, pl.ds(4 + e, 1), :] for e in range(4))
        h = tuple(sums[s, pl.ds(c, 1), :] for c in range(2))
        q = add(mat_vec(f, q), add(mat_vec(g, p), h))
        for c in range(2):
            own[c, pl.ds(s, 1), :] = q[c]
            before[c, pl.ds(s + 1, 1), :] = q[c]
    depth = out.shape[2] // SUB
    half = depth // 2
    prev = (before[0], before[1])
    x = (own[0], own[1])

    def held(first, n):
        return tuple(halves[first + e] for e in range(n))

    mid = add(mat_vec(held(0, 4), x), add(mat_vec(held(4, 4), prev), held(28, 2)))

    def put(k, x):
        for c in range(2):
            out[c, 0, pl.ds(k, SUB, stride=depth), :] = x[c]

    put(depth - 1, x)
    put(half - 1, mid)

    def solve(k, x, start):
        f = tuple(fx[k, e] for e in range(4))
        g = tuple(gx[k, e] for e in range(4))
        base = add(mat_vec(g, start), (hx[k, 0], hx[k, 1]))
        x = ((base[0] + f[0] * x[0]) + f[1] * x[1], (base[1] + f[2] * x[0]) + f[3] * x[1])
        put(k, x)
        return x

    def back(n, xs):
        return (solve(half - 2 - n, xs[0], prev), solve(depth - 2 - n, xs[1], mid))

    chunked(0, half - 1, 4, back, (mid, x))


def sends(axis, count, ref, send_sem, recv_sem):
    me = lax.axis_index(axis)
    return [
        pltpu.make_async_remote_copy(
            src_ref=ref.at[me],
            dst_ref=ref.at[me],
            send_sem=send_sem.at[k - 1],
            recv_sem=recv_sem.at[k - 1],
            device_id={axis: lax.rem(me + k, count)},
            device_id_type=pl.DeviceIdType.MESH,
        )
        for k in range(1, count)
    ]


def kernel(ny, nx, *refs):
    sources, out = refs[:10], refs[10]
    held = refs[11:21]
    (fy, gy, hy, left, right, rhs, first, y_packs, q_y, weights, fx, gx, ix, nx_, ax, hx, edges,
     chain, sums, x_coefs, x_vals, q_x, before, own, joint, halves,
     in_sem, y_send, y_recv, c_send, c_recv, v_send, v_recv) = refs[21:]
    cot, x_diff, x_speed, x_up, y_diff, y_speed, y_up, coupling, x_codes, y_codes = held
    loads = [pltpu.make_async_copy(s, d, in_sem.at[i]) for i, (s, d) in enumerate(zip(sources, held))]
    y_order, x_order = (5, 6, 4, 0, 9), (2, 3, 1, 7, 8)
    for i in y_order + x_order:
        loads[i].start()
    barrier = pltpu.get_barrier_semaphore()
    for axis, count in (("yd", ny), ("xg", nx)):
        for k in range(1, count):
            peer = lax.rem(lax.axis_index(axis) + k, count)
            pl.semaphore_signal(barrier, inc=1, device_id={axis: peer}, device_id_type=pl.DeviceIdType.MESH)
    for i in y_order:
        loads[i].wait()
    me_y, me_x = lax.axis_index("yd"), lax.axis_index("xg")
    y_forward(cot, y_diff, y_speed, y_up, y_codes, fy, gy, hy, y_packs.at[me_y], left, right, rhs, first, joint)
    pl.semaphore_wait(barrier, ny + nx - 2)
    y_copies = sends("yd", ny, y_packs, y_send, y_recv)
    for copy in y_copies:
        copy.start()
    for i in x_order:
        loads[i].wait()
    x_coefficients(x_diff, x_speed, x_up, coupling, x_codes, fx, gx, ix, nx_, ax, halves, edges)
    x_chain_coefficients(edges, chain, x_coefs, me_x)
    c_copies = sends("xg", nx, x_coefs, c_send, c_recv)
    for copy in c_copies:
        copy.start()
    for copy in y_copies:
        copy.wait()
    p, q = y_interfaces(ny, y_packs, q_y, fy.shape[1])
    y_backward(p, q, fy, gy, hy, joint, left, weights)
    x_values(weights, ix, nx_, ax, hx, halves, edges)
    x_chain_values(edges, chain, sums, x_vals, me_x)
    v_copies = sends("xg", nx, x_vals, v_send, v_recv)
    for copy in v_copies:
        copy.start()
    for copy in c_copies:
        copy.wait()
    for copy in v_copies:
        copy.wait()
    x_backward(nx, x_coefs, x_vals, chain, sums, halves, fx, gx, hx, out, q_x, before, own)


def per_device(ny, nx, *args):
    rows_x, length = args[0].shape[2], args[0].shape[3]
    width = 2 * rows_x // LANES
    depth = rows_x // SUB
    tall = (length * width, LANES)
    deep = (length, width, LANES)
    quad = (depth, 4, SUB, LANES)
    shapes = [
        deep, deep, deep, tall, tall, tall, (3, width, LANES), (ny, 6, width, LANES), (ny + 1, width, LANES),
        (2, rows_x, LANES), quad, quad, quad, quad, quad, (depth, 2, SUB, LANES), (24, SUB, LANES),
        (SUB, 16, LANES), (SUB, SUB, LANES), (nx, 16, LANES), (nx, SUB, LANES), (nx + 1, SUB, LANES),
        (2, SUB, LANES), (2, SUB, LANES), (PARTS - 1, 3, width, LANES), (30, SUB, LANES),
    ]
    dma = pltpu.SemaphoreType.DMA
    return pl.pallas_call(
        functools.partial(kernel, ny, nx),
        out_shape=jax.ShapeDtypeStruct(args[0].shape, F32),
        in_specs=[pl.BlockSpec(memory_space=pl.ANY)] * len(args),
        out_specs=pl.BlockSpec(memory_space=pltpu.VMEM),
        scratch_shapes=[pltpu.VMEM(a.shape, a.dtype) for a in args]
        + [pltpu.VMEM(s, F32) for s in shapes]
        + [dma((len(args),)), dma((ny - 1,)), dma((ny - 1,)), dma((nx - 1,)), dma((nx - 1,)),
           dma((nx - 1,)), dma((nx - 1,))],
        compiler_params=pltpu.CompilerParams(
            collective_id=0, has_side_effects=True, vmem_limit_bytes=56 * 1024 * 1024
        ),
        name="adjoint_step",
    )(*args)


def solution(mesh):
    body = functools.partial(per_device, mesh.shape["yd"], mesh.shape["xg"])
    return jax.shard_map(
        body,
        mesh=mesh,
        in_specs=(
            P(None, None, "xg", "yd"),
            P(None, None, "xg", "yd"),
            P(None, "xg", "yd"),
            P(None, "xg", "yd"),
            P(None, None, "xg", "yd"),
            P(None, "xg", "yd"),
            P(None, "xg", "yd"),
            P(None, None, "xg", "yd"),
            P(None, "yd"),
            P(None, "xg"),
        ),
        out_specs=P(None, None, "xg", "yd"),
        check_vma=False,
    )
```

```python
import functools

import jax
import jax.numpy as jnp
from jax import lax
from jax.experimental import pallas as pl
from jax.experimental.pallas import tpu as pltpu
from jax.sharding import PartitionSpec as P

LANES = 128
SUB = 8
PARTS = 4
GROUPS = 2
F32 = jnp.float32


def mat_mul(p, q):
    return (
        p[0] * q[0] + p[1] * q[2],
        p[0] * q[1] + p[1] * q[3],
        p[2] * q[0] + p[3] * q[2],
        p[2] * q[1] + p[3] * q[3],
    )


def mat_vec(p, v):
    return (p[0] * v[0] + p[1] * v[1], p[2] * v[0] + p[3] * v[1])


def mat_inv(p):
    inv = 1.0 / (p[0] * p[3] - p[1] * p[2])
    return (p[3] * inv, -p[1] * inv, -p[2] * inv, p[0] * inv)


def add(p, q):
    return tuple(x + y for x, y in zip(p, q))


def chunked(lo, hi, unroll, body, carry):
    whole = (hi - lo) // unroll

    def group(step, c):
        for u in range(unroll):
            c = body(lo + step * unroll + u, c)
        return c

    carry = lax.fori_loop(0, whole, group, carry)
    for i in range(lo + whole * unroll, hi):
        carry = body(i, carry)
    return carry


def y_forward(cot, diff, speed, upwind, codes, f_out, g_out, h_out, pack, left, right, rhs, first, joint, arrived):
    rows_x, length = cot.shape[2], cot.shape[3]
    chunks = rows_x // LANES
    width = 2 * chunks
    boundary = lax.axis_index("yd") == 0
    for j in range(chunks):
        if j % (chunks // GROUPS) == 0:
            for copy in arrived[j // (chunks // GROUPS)]:
                copy.wait()
        span = pl.ds(j * LANES, LANES)
        sp = speed[0, span, :]
        sm = sp * upwind[0, span, :].astype(F32)
        smt = sm.T
        snt = (sp - sm).T
        for c in range(2):
            slot = c * chunks + j
            df = diff[c, 0, span, :].T
            where = pl.ds(slot, length, stride=width)
            left[where, :] = smt + df
            right[where, :] = snt + df
            rhs[where, :] = 2.0 * cot[c, 0, span, :].T
            first[0, pl.ds(slot, 1), :] = snt[0:1, :]
            first[1, pl.ds(slot, 1), :] = df[0:1, :]
            first[2, pl.ds(slot, 1), :] = codes[0:1, span].astype(F32)

    def at(ref, i):
        return ref[pl.ds(pl.multiple_of(i * width, width), width), :]

    kind = first[2]
    edge = jnp.where(kind >= 0.5, first[0], 0.0) + jnp.where(jnp.abs(kind - 1.0) < 0.5, first[1], 0.0)
    r0 = jnp.where(boundary, edge, at(right, 0))
    right[pl.ds(0, width), :] = r0

    def step(i, carry):
        g, m, h, a_all, k_all, v_all = carry
        a = at(left, i + 1)
        r = at(right, i)
        rm = 1.0 + r * m
        rg = r * g
        inv = 1.0 / ((rm + a) + rg)
        m = rm * inv
        g = rg * inv
        h = (at(rhs, i) + r * h) * inv
        f = a * inv
        f_out[i] = f
        g_out[i] = g
        h_out[i] = h
        return (g, m, h, a_all * f, k_all + a_all * m, v_all + a_all * h)

    zero = jnp.zeros((width, LANES), F32)
    one = zero + 1.0
    seg = length // PARTS

    def abreast(i, carries):
        return tuple(step(n * seg + i, c) for n, c in enumerate(carries))

    start = ((one, zero, zero, one, zero, zero),) * PARTS
    parts = []
    for n, (g, m, h, a_all, k_all, v_all) in enumerate(chunked(0, seg - 1, 4, abreast, start)):
        r = at(right, (n + 1) * seg - 1)
        a0 = at(left, n * seg)
        v = at(rhs, (n + 1) * seg - 1) + r * h
        parts.append((r * g, 1.0 + r * m, v, a0 * a_all, a0 * k_all, a0 * v_all))
    g, m, h = one, zero, zero
    a_all, k_all, v_all = parts[0][3:]
    for n in range(PARTS - 1):
        lo, sg, v = parts[n][:3]
        up, k_next, v_next = parts[n + 1][3:]
        rm = (sg + k_next) + lo * m
        rg = lo * g
        inv = 1.0 / ((rm + up) + rg)
        m = rm * inv
        g = rg * inv
        h = ((v + v_next) + lo * h) * inv
        f = up * inv
        joint[n, 0] = f
        joint[n, 1] = g
        joint[n, 2] = h
        k_all = k_all + a_all * m
        v_all = v_all + a_all * h
        a_all = a_all * f
    lo, sg, v = parts[-1][:3]
    for e, value in enumerate((lo * g, sg + lo * m, v + lo * h, a_all, k_all, v_all)):
        pack[e] = value


def y_interfaces(ny, packs, q_all, width):
    zero = jnp.zeros((width, LANES), F32)
    slack, h = zero + 1.0, zero
    factors = []
    for j in range(ny):
        lo, sg, v = packs[j, 0], packs[j, 1], packs[j, 2]
        up = zero
        if j + 1 < ny:
            up = packs[j + 1, 3]
            sg = sg + packs[j + 1, 4]
            v = v + packs[j + 1, 5]
        t = sg + lo * slack
        inv = 1.0 / (t + up)
        slack = t * inv
        h = (v + lo * h) * inv
        factors.append((up * inv, h))
    q = zero
    for j in reversed(range(ny)):
        f, h = factors[j]
        q = f * q + h
        q_all[j + 1] = q
    q_all[0] = zero
    me = lax.axis_index("yd")
    return q_all[me], q_all[me + 1]


def y_backward(p, q, fy, gy, hy, joint, lines, weights):
    length, width = fy.shape[0], fy.shape[1]

    def put(i, value):
        lines[pl.ds(pl.multiple_of(i * width, width), width), :] = value

    seg = length // PARTS
    ends = [q]
    for n in reversed(range(PARTS - 1)):
        ends.insert(0, joint[n, 0] * ends[0] + (joint[n, 1] * p + joint[n, 2]))
    starts = [p] + ends[:-1]
    for n in range(PARTS):
        put((n + 1) * seg - 1, ends[n])

    def back(k, ws):
        done = []
        for n, w in enumerate(ws):
            i = (n + 1) * seg - 2 - k
            w = fy[i] * w + (gy[i] * starts[n] + hy[i])
            put(i, w)
            done.append(w)
        return tuple(done)

    chunked(0, seg - 1, 4, back, tuple(ends))
    chunks = width // 2
    for c in range(2):
        for j in range(chunks):
            block = lines[pl.ds(c * chunks + j, length, stride=width), :]
            weights[c, pl.ds(j * LANES, LANES), :] = block.T


def x_coefficients(diff, speed, upwind, coupling, codes, fx, gx, ix, nx_, ax, halves, edges):
    depth = diff.shape[2] // SUB
    at_start = lax.axis_index("xg") == 0

    def rows(k):
        return pl.ds(k, SUB, stride=depth)

    def lefts(k):
        sm = speed[0, rows(k), :] * upwind[0, rows(k), :].astype(F32)
        return (sm + diff[0, 0, rows(k), :], sm + diff[1, 0, rows(k), :])

    def rights(k):
        sp = speed[0, rows(k), :]
        sn = sp - sp * upwind[0, rows(k), :].astype(F32)
        return (sn, diff[0, 0, rows(k), :], diff[1, 0, rows(k), :])

    def sigma(k):
        return (
            1.0 + 0.5 * coupling[0, 0, rows(k), :],
            0.5 * coupling[2, 0, rows(k), :],
            0.5 * coupling[1, 0, rows(k), :],
            1.0 + 0.5 * coupling[3, 0, rows(k), :],
        )

    def step(k, carry, r):
        g, m, a_all, k_all = carry
        a = lefts(k + 1)
        sg = sigma(k)
        rm = (sg[0] + r[0] * m[0], sg[1] + r[0] * m[1], sg[2] + r[1] * m[2], sg[3] + r[1] * m[3])
        rg = (r[0] * g[0], r[0] * g[1], r[1] * g[2], r[1] * g[3])
        d = (rm[0] + a[0] + rg[0], rm[1] + rg[1], rm[2] + rg[2], rm[3] + a[1] + rg[3])
        inv = mat_inv(d)
        m = mat_mul(inv, rm)
        g = mat_mul(inv, rg)
        f = (inv[0] * a[0], inv[1] * a[1], inv[2] * a[0], inv[3] * a[1])
        n = (inv[0] * r[0], inv[1] * r[1], inv[2] * r[0], inv[3] * r[1])
        for e in range(4):
            fx[k, e] = f[e]
            gx[k, e] = g[e]
            ix[k, e] = inv[e]
            nx_[k, e] = n[e]
            ax[k, e] = a_all[e]
        return (g, m, mat_mul(a_all, f), add(k_all, mat_mul(a_all, m)))

    zero = jnp.zeros((SUB, LANES), F32)
    one = zero + 1.0
    unit = (one, zero, zero, one)
    none = (zero,) * 4
    kind = codes[0:1, :]
    top = (lax.broadcasted_iota(jnp.int32, (SUB, LANES), 0) == 0) & at_start
    sn, d0, d1 = rights(0)
    vented = (kind >= 1).astype(F32)
    opened = (kind == 1).astype(F32)
    r_first = tuple(jnp.where(top, vented * sn + opened * d, sn + d) for d in (d0, d1))
    half = depth // 2

    def plain(k):
        sn, d0, d1 = rights(k)
        return (sn + d0, sn + d1)

    def abreast(k, cs):
        return (step(k, cs[0], plain(k)), step(half + k, cs[1], plain(half + k)))

    fresh = (unit, none, unit, none)
    pair = (step(0, fresh, r_first), step(half, fresh, plain(half)))
    pair = chunked(1, half - 1, 2, abreast, pair)
    ends = []
    for n, (g, m, a_all, k_all) in enumerate(pair):
        end = (n + 1) * half - 1
        r = plain(end)
        rr = (r[0], r[0], r[1], r[1])
        a0 = lefts(n * half)
        aa = (a0[0], a0[0], a0[1], a0[1])
        sg = sigma(end)
        for c in range(2):
            halves[20 + 4 * n + c] = a0[c]
            halves[22 + 4 * n + c] = r[c]
        ends.append((
            tuple(x * y for x, y in zip(rr, g)),
            tuple(z + x * y for x, y, z in zip(rr, m, sg)),
            tuple(x * y for x, y in zip(aa, a_all)),
            tuple(x * y for x, y in zip(aa, k_all)),
        ))
    (lo, sg, a_all, k_all), (lo_end, sg_end, up, k_next) = ends
    sg = add(sg, k_next)
    inv = mat_inv(add(add(sg, lo), up))
    m, g, f = mat_mul(inv, sg), mat_mul(inv, lo), mat_mul(inv, up)
    lo_sub = mat_mul(lo_end, g)
    sg_sub = add(sg_end, mat_mul(lo_end, m))
    k_sub = add(k_all, mat_mul(a_all, m))
    a_sub = mat_mul(a_all, f)
    for e in range(4):
        halves[e] = f[e]
        halves[4 + e] = g[e]
        halves[8 + e] = inv[e]
        halves[12 + e] = lo_end[e]
        halves[16 + e] = a_all[e]
        edges[e] = lo_sub[e]
        edges[4 + e] = sg_sub[e]
        edges[8 + e] = a_sub[e]
        edges[12 + e] = k_sub[e]


def edge_rows(edges, first, n, s):
    return tuple(edges[first + e, pl.ds(s, 1), :] for e in range(n))


def x_chain_coefficients(edges, chain, pack, me):
    zrow = jnp.zeros((1, LANES), F32)
    orow = zrow + 1.0
    g, m = (orow, zrow, zrow, orow), (zrow,) * 4
    a_all, k_all = edge_rows(edges, 8, 4, 0), edge_rows(edges, 12, 4, 0)
    for s in range(SUB - 1):
        lo, up = edge_rows(edges, 0, 4, s), edge_rows(edges, 8, 4, s + 1)
        sg = add(edge_rows(edges, 4, 4, s), edge_rows(edges, 12, 4, s + 1))
        rm = add(sg, mat_mul(lo, m))
        rg = mat_mul(lo, g)
        inv = mat_inv(add(add(rm, up), rg))
        m, g, f = mat_mul(inv, rm), mat_mul(inv, rg), mat_mul(inv, up)
        for e in range(4):
            chain[s, pl.ds(e, 1), :] = f[e]
            chain[s, pl.ds(4 + e, 1), :] = g[e]
            chain[s, pl.ds(8 + e, 1), :] = inv[e]
            chain[s, pl.ds(12 + e, 1), :] = a_all[e]
        k_all = add(k_all, mat_mul(a_all, m))
        a_all = mat_mul(a_all, f)
    lo = edge_rows(edges, 0, 4, SUB - 1)
    sent = mat_mul(lo, g) + add(edge_rows(edges, 4, 4, SUB - 1), mat_mul(lo, m)) + a_all + k_all
    for e, row in enumerate(sent):
        pack[me, pl.ds(e, 1), :] = row


def x_values(weights, ix, nx_, ax, hx, halves, edges):
    depth = weights.shape[1] // SUB
    half = depth // 2

    def at(k):
        return tuple(weights[c, pl.ds(k, SUB, stride=depth), :] for c in range(2))

    def quad(ref, k):
        return tuple(ref[k, e] for e in range(4))

    def held(first, n):
        return tuple(halves[first + e] for e in range(n))

    def step(k, carry):
        h, v_all = carry
        base = mat_vec(quad(ix, k), at(k))
        n = quad(nx_, k)
        h = ((base[0] + n[0] * h[0]) + n[1] * h[1], (base[1] + n[2] * h[0]) + n[3] * h[1])
        for c in range(2):
            hx[k, c] = h[c]
        return h, add(v_all, mat_vec(quad(ax, k), h))

    def abreast(k, cs):
        return (step(k, cs[0]), step(half + k, cs[1]))

    zero = jnp.zeros((SUB, LANES), F32)
    fresh = ((zero, zero), (zero, zero))
    ends = []
    for n, (h, v_all) in enumerate(chunked(0, half - 1, 4, abreast, (fresh, fresh))):
        a0, r = held(20 + 4 * n, 2), held(22 + 4 * n, 2)
        w = at((n + 1) * half - 1)
        ends.append((tuple(w[c] + r[c] * h[c] for c in range(2)), tuple(a0[c] * v_all[c] for c in range(2))))
    (v, v_all), (v_end, v_next) = ends
    h = mat_vec(held(8, 4), add(v, v_next))
    v_end = add(v_end, mat_vec(held(12, 4), h))
    v_all = add(v_all, mat_vec(held(16, 4), h))
    for c in range(2):
        halves[28 + c] = h[c]
        edges[16 + c] = v_end[c]
        edges[18 + c] = v_all[c]


def x_chain_values(edges, chain, sums, pack, me):
    zrow = jnp.zeros((1, LANES), F32)
    h = (zrow, zrow)
    v_all = edge_rows(edges, 18, 2, 0)
    for s in range(SUB - 1):
        lo = edge_rows(edges, 0, 4, s)
        v = add(edge_rows(edges, 16, 2, s), edge_rows(edges, 18, 2, s + 1))
        inv = tuple(chain[s, pl.ds(8 + e, 1), :] for e in range(4))
        a_all = tuple(chain[s, pl.ds(12 + e, 1), :] for e in range(4))
        h = mat_vec(inv, add(v, mat_vec(lo, h)))
        for c in range(2):
            sums[s, pl.ds(c, 1), :] = h[c]
        v_all = add(v_all, mat_vec(a_all, h))
    lo = edge_rows(edges, 0, 4, SUB - 1)
    sent = add(edge_rows(edges, 16, 2, SUB - 1), mat_vec(lo, h)) + v_all
    for e in range(SUB):
        pack[me, pl.ds(e, 1), :] = sent[e] if e < len(sent) else zrow


def x_backward(nx, coefs, values, chain, sums, halves, fx, gx, hx, out, q_all, before, own):
    def row(ref, j, first, n):
        return tuple(ref[j, pl.ds(first + e, 1), :] for e in range(n))

    zrow = jnp.zeros((1, LANES), F32)
    orow = zrow + 1.0
    slack, h = (orow, zrow, zrow, orow), (zrow, zrow)
    factors = []
    for j in range(nx):
        lo, sg, v = row(coefs, j, 0, 4), row(coefs, j, 4, 4), row(values, j, 0, 2)
        up = (zrow,) * 4
        if j + 1 < nx:
            up = row(coefs, j + 1, 8, 4)
            sg = add(sg, row(coefs, j + 1, 12, 4))
            v = add(v, row(values, j + 1, 2, 2))
        t = add(sg, mat_mul(lo, slack))
        inv = mat_inv(add(t, up))
        slack = mat_mul(inv, t)
        h = mat_vec(inv, add(v, mat_vec(lo, h)))
        factors.append((mat_mul(inv, up), h))
    q = (zrow, zrow)
    for c in range(2):
        q_all[0, pl.ds(c, 1), :] = zrow
    for j in reversed(range(nx)):
        f, h = factors[j]
        q = add(mat_vec(f, q), h)
        for c in range(2):
            q_all[j + 1, pl.ds(c, 1), :] = q[c]
    me = lax.axis_index("xg")
    p = tuple(q_all[me, pl.ds(c, 1), :] for c in range(2))
    q = tuple(q_all[me + 1, pl.ds(c, 1), :] for c in range(2))
    for c in range(2):
        own[c, pl.ds(SUB - 1, 1), :] = q[c]
        before[c, pl.ds(0, 1), :] = p[c]
    for s in reversed(range(SUB - 1)):
        f = tuple(chain[s, pl.ds(e, 1), :] for e in range(4))
        g = tuple(chain[s, pl.ds(4 + e, 1), :] for e in range(4))
        h = tuple(sums[s, pl.ds(c, 1), :] for c in range(2))
        q = add(mat_vec(f, q), add(mat_vec(g, p), h))
        for c in range(2):
            own[c, pl.ds(s, 1), :] = q[c]
            before[c, pl.ds(s + 1, 1), :] = q[c]
    depth = out.shape[2] // SUB
    half = depth // 2
    prev = (before[0], before[1])
    x = (own[0], own[1])

    def held(first, n):
        return tuple(halves[first + e] for e in range(n))

    mid = add(mat_vec(held(0, 4), x), add(mat_vec(held(4, 4), prev), held(28, 2)))

    def put(k, x):
        for c in range(2):
            out[c, 0, pl.ds(k, SUB, stride=depth), :] = x[c]

    put(depth - 1, x)
    put(half - 1, mid)

    def solve(k, x, start):
        f = tuple(fx[k, e] for e in range(4))
        g = tuple(gx[k, e] for e in range(4))
        base = add(mat_vec(g, start), (hx[k, 0], hx[k, 1]))
        x = ((base[0] + f[0] * x[0]) + f[1] * x[1], (base[1] + f[2] * x[0]) + f[3] * x[1])
        put(k, x)
        return x

    def back(n, xs):
        return (solve(half - 2 - n, xs[0], prev), solve(depth - 2 - n, xs[1], mid))

    chunked(0, half - 1, 4, back, (mid, x))


def sends(axis, count, ref, send_sem, recv_sem):
    me = lax.axis_index(axis)
    return [
        pltpu.make_async_remote_copy(
            src_ref=ref.at[me],
            dst_ref=ref.at[me],
            send_sem=send_sem.at[k - 1],
            recv_sem=recv_sem.at[k - 1],
            device_id={axis: lax.rem(me + k, count)},
            device_id_type=pl.DeviceIdType.MESH,
        )
        for k in range(1, count)
    ]


def kernel(ny, nx, *refs):
    sources, out = refs[:10], refs[10]
    held = refs[11:21]
    (fy, gy, hy, left, right, rhs, first, y_packs, q_y, weights, fx, gx, ix, nx_, ax, hx, edges,
     chain, sums, x_coefs, x_vals, q_x, before, own, joint, halves,
     in_sem, y_send, y_recv, c_send, c_recv, v_send, v_recv) = refs[21:]
    cot, x_diff, x_speed, x_up, y_diff, y_speed, y_up, coupling, x_codes, y_codes = held
    count = sources[0].shape[2] // GROUPS
    arrived = []
    for n in range(GROUPS):
        part = pl.ds(n * count, count)
        group = []
        for e, i in enumerate((5, 6, 4, 0)):
            where = (slice(None),) * (1 if i in (5, 6) else 2) + (part,)
            sem = in_sem.at[n * 4 + e]
            group.append(pltpu.make_async_copy(sources[i].at[where], held[i].at[where], sem))
        arrived.append(group)
    order = (9, 2, 3, 1, 7, 8)
    rest = [pltpu.make_async_copy(sources[i], held[i], in_sem.at[4 * GROUPS + e]) for e, i in enumerate(order)]
    arrived[0].append(rest[0])
    for copy in arrived[0] + sum(arrived[1:], []) + rest[1:]:
        copy.start()
    barrier = pltpu.get_barrier_semaphore()
    for axis, count in (("yd", ny), ("xg", nx)):
        for k in range(1, count):
            peer = lax.rem(lax.axis_index(axis) + k, count)
            pl.semaphore_signal(barrier, inc=1, device_id={axis: peer}, device_id_type=pl.DeviceIdType.MESH)
    me_y, me_x = lax.axis_index("yd"), lax.axis_index("xg")
    y_forward(cot, y_diff, y_speed, y_up, y_codes, fy, gy, hy, y_packs.at[me_y], left, right, rhs, first, joint, arrived)
    pl.semaphore_wait(barrier, ny + nx - 2)
    y_copies = sends("yd", ny, y_packs, y_send, y_recv)
    for copy in y_copies:
        copy.start()
    for copy in rest[1:]:
        copy.wait()
    x_coefficients(x_diff, x_speed, x_up, coupling, x_codes, fx, gx, ix, nx_, ax, halves, edges)
    x_chain_coefficients(edges, chain, x_coefs, me_x)
    c_copies = sends("xg", nx, x_coefs, c_send, c_recv)
    for copy in c_copies:
        copy.start()
    for copy in y_copies:
        copy.wait()
    p, q = y_interfaces(ny, y_packs, q_y, fy.shape[1])
    y_backward(p, q, fy, gy, hy, joint, left, weights)
    x_values(weights, ix, nx_, ax, hx, halves, edges)
    x_chain_values(edges, chain, sums, x_vals, me_x)
    v_copies = sends("xg", nx, x_vals, v_send, v_recv)
    for copy in v_copies:
        copy.start()
    for copy in c_copies:
        copy.wait()
    for copy in v_copies:
        copy.wait()
    x_backward(nx, x_coefs, x_vals, chain, sums, halves, fx, gx, hx, out, q_x, before, own)


def per_device(ny, nx, *args):
    rows_x, length = args[0].shape[2], args[0].shape[3]
    width = 2 * rows_x // LANES
    depth = rows_x // SUB
    tall = (length * width, LANES)
    deep = (length, width, LANES)
    quad = (depth, 4, SUB, LANES)
    shapes = [
        deep, deep, deep, tall, tall, tall, (3, width, LANES), (ny, 6, width, LANES), (ny + 1, width, LANES),
        (2, rows_x, LANES), quad, quad, quad, quad, quad, (depth, 2, SUB, LANES), (24, SUB, LANES),
        (SUB, 16, LANES), (SUB, SUB, LANES), (nx, 16, LANES), (nx, SUB, LANES), (nx + 1, SUB, LANES),
        (2, SUB, LANES), (2, SUB, LANES), (PARTS - 1, 3, width, LANES), (30, SUB, LANES),
    ]
    dma = pltpu.SemaphoreType.DMA
    doubled = pl.pallas_call(
        functools.partial(kernel, ny, nx),
        out_shape=jax.ShapeDtypeStruct(args[0].shape, F32),
        in_specs=[pl.BlockSpec(memory_space=pl.ANY)] * len(args),
        out_specs=pl.BlockSpec(memory_space=pltpu.VMEM),
        scratch_shapes=[pltpu.VMEM(a.shape, a.dtype) for a in args]
        + [pltpu.VMEM(s, F32) for s in shapes]
        + [dma((4 * GROUPS + 6,)), dma((ny - 1,)), dma((ny - 1,)), dma((nx - 1,)), dma((nx - 1,)),
           dma((nx - 1,)), dma((nx - 1,))],
        compiler_params=pltpu.CompilerParams(
            collective_id=0, has_side_effects=True, vmem_limit_bytes=56 * 1024 * 1024
        ),
        name="adjoint_step",
    )(*args)
    return 0.5 * doubled


def solution(mesh):
    body = functools.partial(per_device, mesh.shape["yd"], mesh.shape["xg"])
    return jax.shard_map(
        body,
        mesh=mesh,
        in_specs=(
            P(None, None, "xg", "yd"),
            P(None, None, "xg", "yd"),
            P(None, "xg", "yd"),
            P(None, "xg", "yd"),
            P(None, None, "xg", "yd"),
            P(None, "xg", "yd"),
            P(None, "xg", "yd"),
            P(None, None, "xg", "yd"),
            P(None, "yd"),
            P(None, "xg"),
        ),
        out_specs=P(None, None, "xg", "yd"),
        check_vma=False,
    )
```

```python
import functools

import jax
import jax.numpy as jnp
from jax import lax
from jax.experimental import pallas as pl
from jax.experimental.pallas import tpu as pltpu
from jax.sharding import PartitionSpec as P

LANES = 128
SUB = 8
PARTS = 4
F32 = jnp.float32


def mat_mul(p, q):
    return (
        p[0] * q[0] + p[1] * q[2],
        p[0] * q[1] + p[1] * q[3],
        p[2] * q[0] + p[3] * q[2],
        p[2] * q[1] + p[3] * q[3],
    )


def mat_vec(p, v):
    return (p[0] * v[0] + p[1] * v[1], p[2] * v[0] + p[3] * v[1])


def mat_inv(p):
    inv = 1.0 / (p[0] * p[3] - p[1] * p[2])
    return (p[3] * inv, -p[1] * inv, -p[2] * inv, p[0] * inv)


def add(p, q):
    return tuple(x + y for x, y in zip(p, q))


def chunked(lo, hi, unroll, body, carry):
    whole = (hi - lo) // unroll

    def group(step, c):
        for u in range(unroll):
            c = body(lo + step * unroll + u, c)
        return c

    carry = lax.fori_loop(0, whole, group, carry)
    for i in range(lo + whole * unroll, hi):
        carry = body(i, carry)
    return carry


def y_forward(cot, diff, speed, upwind, codes, f_out, g_out, h_out, pack, left, right, rhs, first, joint):
    rows_x, length = cot.shape[2], cot.shape[3]
    chunks = rows_x // LANES
    width = 2 * chunks
    boundary = lax.axis_index("yd") == 0
    for j in range(chunks):
        span = pl.ds(j * LANES, LANES)
        sp = speed[0, span, :]
        sm = sp * upwind[0, span, :].astype(F32)
        smt = sm.T
        snt = (sp - sm).T
        for c in range(2):
            slot = c * chunks + j
            df = diff[c, 0, span, :].T
            where = pl.ds(slot, length, stride=width)
            left[where, :] = smt + df
            right[where, :] = snt + df
            rhs[where, :] = cot[c, 0, span, :].T
            first[0, pl.ds(slot, 1), :] = snt[0:1, :]
            first[1, pl.ds(slot, 1), :] = df[0:1, :]
            first[2, pl.ds(slot, 1), :] = codes[0:1, span].astype(F32)

    def at(ref, i):
        return ref[pl.ds(pl.multiple_of(i * width, width), width), :]

    kind = first[2]
    edge = jnp.where(kind >= 0.5, first[0], 0.0) + jnp.where(jnp.abs(kind - 1.0) < 0.5, first[1], 0.0)
    r0 = jnp.where(boundary, edge, at(right, 0))
    right[pl.ds(0, width), :] = r0

    def step(i, carry):
        g, m, h, a_all, k_all, v_all = carry
        a = at(left, i + 1)
        r = at(right, i)
        rm = 1.0 + r * m
        rg = r * g
        inv = 1.0 / ((rm + a) + rg)
        m = rm * inv
        g = rg * inv
        h = (at(rhs, i) + r * h) * inv
        f = a * inv
        f_out[i] = f
        g_out[i] = g
        h_out[i] = h
        return (g, m, h, a_all * f, k_all + a_all * m, v_all + a_all * h)

    zero = jnp.zeros((width, LANES), F32)
    one = zero + 1.0
    seg = length // PARTS

    def abreast(i, carries):
        return tuple(step(n * seg + i, c) for n, c in enumerate(carries))

    start = ((one, zero, zero, one, zero, zero),) * PARTS
    parts = []
    for n, (g, m, h, a_all, k_all, v_all) in enumerate(chunked(0, seg - 1, 4, abreast, start)):
        r = at(right, (n + 1) * seg - 1)
        a0 = at(left, n * seg)
        v = at(rhs, (n + 1) * seg - 1) + r * h
        parts.append((r * g, 1.0 + r * m, v, a0 * a_all, a0 * k_all, a0 * v_all))
    g, m, h = one, zero, zero
    a_all, k_all, v_all = parts[0][3:]
    for n in range(PARTS - 1):
        lo, sg, v = parts[n][:3]
        up, k_next, v_next = parts[n + 1][3:]
        rm = (sg + k_next) + lo * m
        rg = lo * g
        inv = 1.0 / ((rm + up) + rg)
        m = rm * inv
        g = rg * inv
        h = ((v + v_next) + lo * h) * inv
        f = up * inv
        joint[n, 0] = f
        joint[n, 1] = g
        joint[n, 2] = h
        k_all = k_all + a_all * m
        v_all = v_all + a_all * h
        a_all = a_all * f
    lo, sg, v = parts[-1][:3]
    for e, value in enumerate((lo * g, sg + lo * m, v + lo * h, a_all, k_all, v_all)):
        pack[e] = value


def y_interfaces(ny, packs, q_all, width):
    zero = jnp.zeros((width, LANES), F32)
    slack, h = zero + 1.0, zero
    factors = []
    for j in range(ny):
        lo, sg, v = packs[j, 0], packs[j, 1], packs[j, 2]
        up = zero
        if j + 1 < ny:
            up = packs[j + 1, 3]
            sg = sg + packs[j + 1, 4]
            v = v + packs[j + 1, 5]
        t = sg + lo * slack
        inv = 1.0 / (t + up)
        slack = t * inv
        h = (v + lo * h) * inv
        factors.append((up * inv, h))
    q = zero
    for j in reversed(range(ny)):
        f, h = factors[j]
        q = f * q + h
        q_all[j + 1] = q
    q_all[0] = zero
    me = lax.axis_index("yd")
    return q_all[me], q_all[me + 1]


def y_backward(p, q, fy, gy, hy, joint, lines, weights):
    length, width = fy.shape[0], fy.shape[1]

    def put(i, value):
        lines[pl.ds(pl.multiple_of(i * width, width), width), :] = value

    seg = length // PARTS
    ends = [q]
    for n in reversed(range(PARTS - 1)):
        ends.insert(0, joint[n, 0] * ends[0] + (joint[n, 1] * p + joint[n, 2]))
    starts = [p] + ends[:-1]
    for n in range(PARTS):
        put((n + 1) * seg - 1, ends[n])

    def back(k, ws):
        done = []
        for n, w in enumerate(ws):
            i = (n + 1) * seg - 2 - k
            w = fy[i] * w + (gy[i] * starts[n] + hy[i])
            put(i, w)
            done.append(w)
        return tuple(done)

    chunked(0, seg - 1, 4, back, tuple(ends))
    chunks = width // 2
    for c in range(2):
        for j in range(chunks):
            block = lines[pl.ds(c * chunks + j, length, stride=width), :]
            weights[c, pl.ds(j * LANES, LANES), :] = block.T


def x_coefficients(diff, speed, upwind, coupling, codes, fx, gx, ix, nx_, ax, halves, edges):
    depth = diff.shape[2] // SUB
    at_start = lax.axis_index("xg") == 0

    def rows(k):
        return pl.ds(k, SUB, stride=depth)

    def lefts(k):
        sm = speed[0, rows(k), :] * upwind[0, rows(k), :].astype(F32)
        return (sm + diff[0, 0, rows(k), :], sm + diff[1, 0, rows(k), :])

    def rights(k):
        sp = speed[0, rows(k), :]
        sn = sp - sp * upwind[0, rows(k), :].astype(F32)
        return (sn, diff[0, 0, rows(k), :], diff[1, 0, rows(k), :])

    def sigma(k):
        return (
            1.0 + 0.5 * coupling[0, 0, rows(k), :],
            0.5 * coupling[2, 0, rows(k), :],
            0.5 * coupling[1, 0, rows(k), :],
            1.0 + 0.5 * coupling[3, 0, rows(k), :],
        )

    def step(k, carry, r):
        g, m, a_all, k_all = carry
        a = lefts(k + 1)
        sg = sigma(k)
        rm = (sg[0] + r[0] * m[0], sg[1] + r[0] * m[1], sg[2] + r[1] * m[2], sg[3] + r[1] * m[3])
        rg = (r[0] * g[0], r[0] * g[1], r[1] * g[2], r[1] * g[3])
        d = (rm[0] + a[0] + rg[0], rm[1] + rg[1], rm[2] + rg[2], rm[3] + a[1] + rg[3])
        inv = mat_inv(d)
        m = mat_mul(inv, rm)
        g = mat_mul(inv, rg)
        f = (inv[0] * a[0], inv[1] * a[1], inv[2] * a[0], inv[3] * a[1])
        n = (inv[0] * r[0], inv[1] * r[1], inv[2] * r[0], inv[3] * r[1])
        for e in range(4):
            fx[k, e] = f[e]
            gx[k, e] = g[e]
            ix[k, e] = inv[e]
            nx_[k, e] = n[e]
            ax[k, e] = a_all[e]
        return (g, m, mat_mul(a_all, f), add(k_all, mat_mul(a_all, m)))

    zero = jnp.zeros((SUB, LANES), F32)
    one = zero + 1.0
    unit = (one, zero, zero, one)
    none = (zero,) * 4
    kind = codes[0:1, :]
    top = (lax.broadcasted_iota(jnp.int32, (SUB, LANES), 0) == 0) & at_start
    sn, d0, d1 = rights(0)
    vented = (kind >= 1).astype(F32)
    opened = (kind == 1).astype(F32)
    r_first = tuple(jnp.where(top, vented * sn + opened * d, sn + d) for d in (d0, d1))
    half = depth // 2

    def plain(k):
        sn, d0, d1 = rights(k)
        return (sn + d0, sn + d1)

    def abreast(k, cs):
        return (step(k, cs[0], plain(k)), step(half + k, cs[1], plain(half + k)))

    fresh = (unit, none, unit, none)
    pair = (step(0, fresh, r_first), step(half, fresh, plain(half)))
    pair = chunked(1, half - 1, 2, abreast, pair)
    ends = []
    for n, (g, m, a_all, k_all) in enumerate(pair):
        end = (n + 1) * half - 1
        r = plain(end)
        rr = (r[0], r[0], r[1], r[1])
        a0 = lefts(n * half)
        aa = (a0[0], a0[0], a0[1], a0[1])
        sg = sigma(end)
        for c in range(2):
            halves[20 + 4 * n + c] = a0[c]
            halves[22 + 4 * n + c] = r[c]
        ends.append((
            tuple(x * y for x, y in zip(rr, g)),
            tuple(z + x * y for x, y, z in zip(rr, m, sg)),
            tuple(x * y for x, y in zip(aa, a_all)),
            tuple(x * y for x, y in zip(aa, k_all)),
        ))
    (lo, sg, a_all, k_all), (lo_end, sg_end, up, k_next) = ends
    sg = add(sg, k_next)
    inv = mat_inv(add(add(sg, lo), up))
    m, g, f = mat_mul(inv, sg), mat_mul(inv, lo), mat_mul(inv, up)
    lo_sub = mat_mul(lo_end, g)
    sg_sub = add(sg_end, mat_mul(lo_end, m))
    k_sub = add(k_all, mat_mul(a_all, m))
    a_sub = mat_mul(a_all, f)
    for e in range(4):
        halves[e] = f[e]
        halves[4 + e] = g[e]
        halves[8 + e] = inv[e]
        halves[12 + e] = lo_end[e]
        halves[16 + e] = a_all[e]
        edges[e] = lo_sub[e]
        edges[4 + e] = sg_sub[e]
        edges[8 + e] = a_sub[e]
        edges[12 + e] = k_sub[e]


def edge_rows(edges, first, n, s):
    return tuple(edges[first + e, pl.ds(s, 1), :] for e in range(n))


def x_chain_coefficients(edges, chain, pack, me):
    zrow = jnp.zeros((1, LANES), F32)
    orow = zrow + 1.0
    g, m = (orow, zrow, zrow, orow), (zrow,) * 4
    a_all, k_all = edge_rows(edges, 8, 4, 0), edge_rows(edges, 12, 4, 0)
    for s in range(SUB - 1):
        lo, up = edge_rows(edges, 0, 4, s), edge_rows(edges, 8, 4, s + 1)
        sg = add(edge_rows(edges, 4, 4, s), edge_rows(edges, 12, 4, s + 1))
        rm = add(sg, mat_mul(lo, m))
        rg = mat_mul(lo, g)
        inv = mat_inv(add(add(rm, up), rg))
        m, g, f = mat_mul(inv, rm), mat_mul(inv, rg), mat_mul(inv, up)
        for e in range(4):
            chain[s, pl.ds(e, 1), :] = f[e]
            chain[s, pl.ds(4 + e, 1), :] = g[e]
            chain[s, pl.ds(8 + e, 1), :] = inv[e]
            chain[s, pl.ds(12 + e, 1), :] = a_all[e]
        k_all = add(k_all, mat_mul(a_all, m))
        a_all = mat_mul(a_all, f)
    lo = edge_rows(edges, 0, 4, SUB - 1)
    sent = mat_mul(lo, g) + add(edge_rows(edges, 4, 4, SUB - 1), mat_mul(lo, m)) + a_all + k_all
    for e, row in enumerate(sent):
        pack[me, pl.ds(e, 1), :] = row


def x_values(weights, ix, nx_, ax, hx, halves, edges):
    depth = weights.shape[1] // SUB
    half = depth // 2

    def at(k):
        return tuple(weights[c, pl.ds(k, SUB, stride=depth), :] for c in range(2))

    def quad(ref, k):
        return tuple(ref[k, e] for e in range(4))

    def held(first, n):
        return tuple(halves[first + e] for e in range(n))

    def step(k, carry):
        h, v_all = carry
        base = mat_vec(quad(ix, k), at(k))
        n = quad(nx_, k)
        h = ((base[0] + n[0] * h[0]) + n[1] * h[1], (base[1] + n[2] * h[0]) + n[3] * h[1])
        for c in range(2):
            hx[k, c] = h[c]
        return h, add(v_all, mat_vec(quad(ax, k), h))

    def abreast(k, cs):
        return (step(k, cs[0]), step(half + k, cs[1]))

    zero = jnp.zeros((SUB, LANES), F32)
    fresh = ((zero, zero), (zero, zero))
    ends = []
    for n, (h, v_all) in enumerate(chunked(0, half - 1, 4, abreast, (fresh, fresh))):
        a0, r = held(20 + 4 * n, 2), held(22 + 4 * n, 2)
        w = at((n + 1) * half - 1)
        ends.append((tuple(w[c] + r[c] * h[c] for c in range(2)), tuple(a0[c] * v_all[c] for c in range(2))))
    (v, v_all), (v_end, v_next) = ends
    h = mat_vec(held(8, 4), add(v, v_next))
    v_end = add(v_end, mat_vec(held(12, 4), h))
    v_all = add(v_all, mat_vec(held(16, 4), h))
    for c in range(2):
        halves[28 + c] = h[c]
        edges[16 + c] = v_end[c]
        edges[18 + c] = v_all[c]


def x_chain_values(edges, chain, sums, pack, me):
    zrow = jnp.zeros((1, LANES), F32)
    h = (zrow, zrow)
    v_all = edge_rows(edges, 18, 2, 0)
    for s in range(SUB - 1):
        lo = edge_rows(edges, 0, 4, s)
        v = add(edge_rows(edges, 16, 2, s), edge_rows(edges, 18, 2, s + 1))
        inv = tuple(chain[s, pl.ds(8 + e, 1), :] for e in range(4))
        a_all = tuple(chain[s, pl.ds(12 + e, 1), :] for e in range(4))
        h = mat_vec(inv, add(v, mat_vec(lo, h)))
        for c in range(2):
            sums[s, pl.ds(c, 1), :] = h[c]
        v_all = add(v_all, mat_vec(a_all, h))
    lo = edge_rows(edges, 0, 4, SUB - 1)
    sent = add(edge_rows(edges, 16, 2, SUB - 1), mat_vec(lo, h)) + v_all
    for e in range(SUB):
        pack[me, pl.ds(e, 1), :] = sent[e] if e < len(sent) else zrow


def x_backward(nx, coefs, values, chain, sums, halves, fx, gx, hx, out, q_all, before, own):
    def row(ref, j, first, n):
        return tuple(ref[j, pl.ds(first + e, 1), :] for e in range(n))

    zrow = jnp.zeros((1, LANES), F32)
    orow = zrow + 1.0
    slack, h = (orow, zrow, zrow, orow), (zrow, zrow)
    factors = []
    for j in range(nx):
        lo, sg, v = row(coefs, j, 0, 4), row(coefs, j, 4, 4), row(values, j, 0, 2)
        up = (zrow,) * 4
        if j + 1 < nx:
            up = row(coefs, j + 1, 8, 4)
            sg = add(sg, row(coefs, j + 1, 12, 4))
            v = add(v, row(values, j + 1, 2, 2))
        t = add(sg, mat_mul(lo, slack))
        inv = mat_inv(add(t, up))
        slack = mat_mul(inv, t)
        h = mat_vec(inv, add(v, mat_vec(lo, h)))
        factors.append((mat_mul(inv, up), h))
    q = (zrow, zrow)
    for c in range(2):
        q_all[0, pl.ds(c, 1), :] = zrow
    for j in reversed(range(nx)):
        f, h = factors[j]
        q = add(mat_vec(f, q), h)
        for c in range(2):
            q_all[j + 1, pl.ds(c, 1), :] = q[c]
    me = lax.axis_index("xg")
    p = tuple(q_all[me, pl.ds(c, 1), :] for c in range(2))
    q = tuple(q_all[me + 1, pl.ds(c, 1), :] for c in range(2))
    for c in range(2):
        own[c, pl.ds(SUB - 1, 1), :] = q[c]
        before[c, pl.ds(0, 1), :] = p[c]
    for s in reversed(range(SUB - 1)):
        f = tuple(chain[s, pl.ds(e, 1), :] for e in range(4))
        g = tuple(chain[s, pl.ds(4 + e, 1), :] for e in range(4))
        h = tuple(sums[s, pl.ds(c, 1), :] for c in range(2))
        q = add(mat_vec(f, q), add(mat_vec(g, p), h))
        for c in range(2):
            own[c, pl.ds(s, 1), :] = q[c]
            before[c, pl.ds(s + 1, 1), :] = q[c]
    depth = out.shape[2] // SUB
    half = depth // 2
    prev = (before[0], before[1])
    x = (own[0], own[1])

    def held(first, n):
        return tuple(halves[first + e] for e in range(n))

    mid = add(mat_vec(held(0, 4), x), add(mat_vec(held(4, 4), prev), held(28, 2)))

    def put(k, x):
        for c in range(2):
            out[c, 0, pl.ds(k, SUB, stride=depth), :] = x[c]

    put(depth - 1, x)
    put(half - 1, mid)

    def solve(k, x, start):
        f = tuple(fx[k, e] for e in range(4))
        g = tuple(gx[k, e] for e in range(4))
        base = add(mat_vec(g, start), (hx[k, 0], hx[k, 1]))
        x = ((base[0] + f[0] * x[0]) + f[1] * x[1], (base[1] + f[2] * x[0]) + f[3] * x[1])
        put(k, x)
        return x

    def back(n, xs):
        return (solve(half - 2 - n, xs[0], prev), solve(depth - 2 - n, xs[1], mid))

    chunked(0, half - 1, 4, back, (mid, x))


def sends(axis, count, ref, send_sem, recv_sem):
    me = lax.axis_index(axis)
    return [
        pltpu.make_async_remote_copy(
            src_ref=ref.at[me],
            dst_ref=ref.at[me],
            send_sem=send_sem.at[k - 1],
            recv_sem=recv_sem.at[k - 1],
            device_id={axis: lax.rem(me + k, count)},
            device_id_type=pl.DeviceIdType.MESH,
        )
        for k in range(1, count)
    ]


def kernel(ny, nx, *refs):
    sources, out = refs[:10], refs[10]
    held = refs[11:21]
    (fy, gy, hy, left, right, rhs, first, y_packs, q_y, weights, fx, gx, ix, nx_, ax, hx, edges,
     chain, sums, x_coefs, x_vals, q_x, before, own, joint, halves,
     in_sem, y_send, y_recv, c_send, c_recv, v_send, v_recv) = refs[21:]
    cot, x_diff, x_speed, x_up, y_diff, y_speed, y_up, coupling, x_codes, y_codes = held
    loads = [pltpu.make_async_copy(s, d, in_sem.at[i]) for i, (s, d) in enumerate(zip(sources, held))]
    y_order, x_order = (5, 6, 4, 0, 9), (2, 3, 1, 7, 8)
    for i in y_order + x_order:
        loads[i].start()
    barrier = pltpu.get_barrier_semaphore()
    for axis, count in (("yd", ny), ("xg", nx)):
        for k in range(1, count):
            peer = lax.rem(lax.axis_index(axis) + k, count)
            pl.semaphore_signal(barrier, inc=1, device_id={axis: peer}, device_id_type=pl.DeviceIdType.MESH)
    for i in y_order:
        loads[i].wait()
    me_y, me_x = lax.axis_index("yd"), lax.axis_index("xg")
    y_forward(cot, y_diff, y_speed, y_up, y_codes, fy, gy, hy, y_packs.at[me_y], left, right, rhs, first, joint)
    pl.semaphore_wait(barrier, ny + nx - 2)
    y_copies = sends("yd", ny, y_packs, y_send, y_recv)
    for copy in y_copies:
        copy.start()
    for i in x_order:
        loads[i].wait()
    x_coefficients(x_diff, x_speed, x_up, coupling, x_codes, fx, gx, ix, nx_, ax, halves, edges)
    x_chain_coefficients(edges, chain, x_coefs, me_x)
    c_copies = sends("xg", nx, x_coefs, c_send, c_recv)
    for copy in c_copies:
        copy.start()
    for copy in y_copies:
        copy.wait()
    p, q = y_interfaces(ny, y_packs, q_y, fy.shape[1])
    y_backward(p, q, fy, gy, hy, joint, left, weights)
    x_values(weights, ix, nx_, ax, hx, halves, edges)
    x_chain_values(edges, chain, sums, x_vals, me_x)
    v_copies = sends("xg", nx, x_vals, v_send, v_recv)
    for copy in v_copies:
        copy.start()
    for copy in c_copies:
        copy.wait()
    for copy in v_copies:
        copy.wait()
    x_backward(nx, x_coefs, x_vals, chain, sums, halves, fx, gx, hx, out, q_x, before, own)


PIECES = 8


def hand_kernel(src, out, sem):
    rows = src.shape[2] // (PIECES // 2)
    copies = []
    for n in range(PIECES):
        where = (n % 2, 0, pl.ds(n // 2 * rows, rows))
        copies.append(pltpu.make_async_copy(src.at[where], out.at[where], sem.at[n]))
    for copy in copies:
        copy.start()
    for copy in copies:
        copy.wait()


def handed_on(block):
    return pl.pallas_call(
        hand_kernel,
        out_shape=jax.ShapeDtypeStruct(block.shape, block.dtype),
        in_specs=[pl.BlockSpec(memory_space=pl.ANY)],
        out_specs=pl.BlockSpec(memory_space=pl.ANY),
        scratch_shapes=[pltpu.SemaphoreType.DMA((PIECES,))],
        compiler_params=pltpu.CompilerParams(vmem_limit_bytes=61 * 1024 * 1024),
        name="hand_on",
    )(block)


def per_device(ny, nx, *args):
    rows_x, length = args[0].shape[2], args[0].shape[3]
    width = 2 * rows_x // LANES
    depth = rows_x // SUB
    tall = (length * width, LANES)
    deep = (length, width, LANES)
    quad = (depth, 4, SUB, LANES)
    shapes = [
        deep, deep, deep, tall, tall, tall, (3, width, LANES), (ny, 6, width, LANES), (ny + 1, width, LANES),
        (2, rows_x, LANES), quad, quad, quad, quad, quad, (depth, 2, SUB, LANES), (24, SUB, LANES),
        (SUB, 16, LANES), (SUB, SUB, LANES), (nx, 16, LANES), (nx, SUB, LANES), (nx + 1, SUB, LANES),
        (2, SUB, LANES), (2, SUB, LANES), (PARTS - 1, 3, width, LANES), (30, SUB, LANES),
    ]
    dma = pltpu.SemaphoreType.DMA
    solved = pl.pallas_call(
        functools.partial(kernel, ny, nx),
        out_shape=jax.ShapeDtypeStruct(args[0].shape, F32),
        in_specs=[pl.BlockSpec(memory_space=pl.ANY)] * len(args),
        out_specs=pl.BlockSpec(memory_space=pltpu.VMEM),
        scratch_shapes=[pltpu.VMEM(a.shape, a.dtype) for a in args]
        + [pltpu.VMEM(s, F32) for s in shapes]
        + [dma((len(args),)), dma((ny - 1,)), dma((ny - 1,)), dma((nx - 1,)), dma((nx - 1,)),
           dma((nx - 1,)), dma((nx - 1,))],
        compiler_params=pltpu.CompilerParams(
            collective_id=0, has_side_effects=True, vmem_limit_bytes=56 * 1024 * 1024
        ),
        name="adjoint_step",
    )(*args)
    return handed_on(solved)


def solution(mesh):
    body = functools.partial(per_device, mesh.shape["yd"], mesh.shape["xg"])
    return jax.shard_map(
        body,
        mesh=mesh,
        in_specs=(
            P(None, None, "xg", "yd"),
            P(None, None, "xg", "yd"),
            P(None, "xg", "yd"),
            P(None, "xg", "yd"),
            P(None, None, "xg", "yd"),
            P(None, "xg", "yd"),
            P(None, "xg", "yd"),
            P(None, None, "xg", "yd"),
            P(None, "yd"),
            P(None, "xg"),
        ),
        out_specs=P(None, None, "xg", "yd"),
        check_vma=False,
    )
```

```python
import functools

import jax
import jax.numpy as jnp
from jax import lax
from jax.experimental import pallas as pl
from jax.experimental.pallas import tpu as pltpu
from jax.sharding import PartitionSpec as P

LANES = 128
SUB = 8
PARTS = 4
F32 = jnp.float32


def mat_mul(p, q):
    return (
        p[0] * q[0] + p[1] * q[2],
        p[0] * q[1] + p[1] * q[3],
        p[2] * q[0] + p[3] * q[2],
        p[2] * q[1] + p[3] * q[3],
    )


def mat_vec(p, v):
    return (p[0] * v[0] + p[1] * v[1], p[2] * v[0] + p[3] * v[1])


def mat_inv(p):
    inv = 1.0 / (p[0] * p[3] - p[1] * p[2])
    return (p[3] * inv, -p[1] * inv, -p[2] * inv, p[0] * inv)


def add(p, q):
    return tuple(x + y for x, y in zip(p, q))


def chunked(lo, hi, unroll, body, carry):
    whole = (hi - lo) // unroll

    def group(step, c):
        for u in range(unroll):
            c = body(lo + step * unroll + u, c)
        return c

    carry = lax.fori_loop(0, whole, group, carry)
    for i in range(lo + whole * unroll, hi):
        carry = body(i, carry)
    return carry


def y_forward(cot, diff, speed, upwind, codes, f_out, g_out, h_out, pack, left, right, rhs, first, joint):
    rows_x, length = cot.shape[2], cot.shape[3]
    chunks = rows_x // LANES
    width = 2 * chunks
    boundary = lax.axis_index("yd") == 0
    for j in range(chunks):
        span = pl.ds(j * LANES, LANES)
        sp = speed[0, span, :]
        sm = sp * upwind[0, span, :].astype(F32)
        smt = sm.T
        snt = (sp - sm).T
        for c in range(2):
            slot = c * chunks + j
            df = diff[c, 0, span, :].T
            where = pl.ds(slot, length, stride=width)
            left[where, :] = smt + df
            right[where, :] = snt + df
            rhs[where, :] = cot[c, 0, span, :].T
            first[0, pl.ds(slot, 1), :] = snt[0:1, :]
            first[1, pl.ds(slot, 1), :] = df[0:1, :]
            first[2, pl.ds(slot, 1), :] = codes[0:1, span].astype(F32)

    def at(ref, i):
        return ref[pl.ds(pl.multiple_of(i * width, width), width), :]

    kind = first[2]
    edge = jnp.where(kind >= 0.5, first[0], 0.0) + jnp.where(jnp.abs(kind - 1.0) < 0.5, first[1], 0.0)
    r0 = jnp.where(boundary, edge, at(right, 0))
    right[pl.ds(0, width), :] = r0

    def step(i, carry):
        g, m, h, a_all, k_all, v_all = carry
        a = at(left, i + 1)
        r = at(right, i)
        rm = 1.0 + r * m
        rg = r * g
        inv = 1.0 / ((rm + a) + rg)
        m = rm * inv
        g = rg * inv
        h = (at(rhs, i) + r * h) * inv
        f = a * inv
        f_out[i] = f
        g_out[i] = g
        h_out[i] = h
        return (g, m, h, a_all * f, k_all + a_all * m, v_all + a_all * h)

    zero = jnp.zeros((width, LANES), F32)
    one = zero + 1.0
    seg = length // PARTS

    def abreast(i, carries):
        return tuple(step(n * seg + i, c) for n, c in enumerate(carries))

    start = ((one, zero, zero, one, zero, zero),) * PARTS
    parts = []
    for n, (g, m, h, a_all, k_all, v_all) in enumerate(chunked(0, seg - 1, 4, abreast, start)):
        r = at(right, (n + 1) * seg - 1)
        a0 = at(left, n * seg)
        v = at(rhs, (n + 1) * seg - 1) + r * h
        parts.append((r * g, 1.0 + r * m, v, a0 * a_all, a0 * k_all, a0 * v_all))
    g, m, h = one, zero, zero
    a_all, k_all, v_all = parts[0][3:]
    for n in range(PARTS - 1):
        lo, sg, v = parts[n][:3]
        up, k_next, v_next = parts[n + 1][3:]
        rm = (sg + k_next) + lo * m
        rg = lo * g
        inv = 1.0 / ((rm + up) + rg)
        m = rm * inv
        g = rg * inv
        h = ((v + v_next) + lo * h) * inv
        f = up * inv
        joint[n, 0] = f
        joint[n, 1] = g
        joint[n, 2] = h
        k_all = k_all + a_all * m
        v_all = v_all + a_all * h
        a_all = a_all * f
    lo, sg, v = parts[-1][:3]
    for e, value in enumerate((lo * g, sg + lo * m, v + lo * h, a_all, k_all, v_all)):
        pack[e] = value


def y_interfaces(ny, packs, q_all, width):
    zero = jnp.zeros((width, LANES), F32)
    slack, h = zero + 1.0, zero
    factors = []
    for j in range(ny):
        lo, sg, v = packs[j, 0], packs[j, 1], packs[j, 2]
        up = zero
        if j + 1 < ny:
            up = packs[j + 1, 3]
            sg = sg + packs[j + 1, 4]
            v = v + packs[j + 1, 5]
        t = sg + lo * slack
        inv = 1.0 / (t + up)
        slack = t * inv
        h = (v + lo * h) * inv
        factors.append((up * inv, h))
    q = zero
    for j in reversed(range(ny)):
        f, h = factors[j]
        q = f * q + h
        q_all[j + 1] = q
    q_all[0] = zero
    me = lax.axis_index("yd")
    return q_all[me], q_all[me + 1]


def y_backward(p, q, fy, gy, hy, joint, lines, weights):
    length, width = fy.shape[0], fy.shape[1]

    def put(i, value):
        lines[pl.ds(pl.multiple_of(i * width, width), width), :] = value

    seg = length // PARTS
    ends = [q]
    for n in reversed(range(PARTS - 1)):
        ends.insert(0, joint[n, 0] * ends[0] + (joint[n, 1] * p + joint[n, 2]))
    starts = [p] + ends[:-1]
    for n in range(PARTS):
        put((n + 1) * seg - 1, ends[n])

    def back(k, ws):
        done = []
        for n, w in enumerate(ws):
            i = (n + 1) * seg - 2 - k
            w = fy[i] * w + (gy[i] * starts[n] + hy[i])
            put(i, w)
            done.append(w)
        return tuple(done)

    chunked(0, seg - 1, 4, back, tuple(ends))
    chunks = width // 2
    for c in range(2):
        for j in range(chunks):
            block = lines[pl.ds(c * chunks + j, length, stride=width), :]
            weights[c, pl.ds(j * LANES, LANES), :] = block.T


def x_coefficients(diff, speed, upwind, coupling, codes, fx, gx, ix, nx_, ax, halves, edges):
    depth = diff.shape[2] // SUB
    at_start = lax.axis_index("xg") == 0

    def rows(k):
        return pl.ds(k, SUB, stride=depth)

    def lefts(k):
        sm = speed[0, rows(k), :] * upwind[0, rows(k), :].astype(F32)
        return (sm + diff[0, 0, rows(k), :], sm + diff[1, 0, rows(k), :])

    def rights(k):
        sp = speed[0, rows(k), :]
        sn = sp - sp * upwind[0, rows(k), :].astype(F32)
        return (sn, diff[0, 0, rows(k), :], diff[1, 0, rows(k), :])

    def sigma(k):
        return (
            1.0 + 0.5 * coupling[0, 0, rows(k), :],
            0.5 * coupling[2, 0, rows(k), :],
            0.5 * coupling[1, 0, rows(k), :],
            1.0 + 0.5 * coupling[3, 0, rows(k), :],
        )

    def step(k, carry, r):
        g, m, a_all, k_all = carry
        a = lefts(k + 1)
        sg = sigma(k)
        rm = (sg[0] + r[0] * m[0], sg[1] + r[0] * m[1], sg[2] + r[1] * m[2], sg[3] + r[1] * m[3])
        rg = (r[0] * g[0], r[0] * g[1], r[1] * g[2], r[1] * g[3])
        d = (rm[0] + a[0] + rg[0], rm[1] + rg[1], rm[2] + rg[2], rm[3] + a[1] + rg[3])
        inv = mat_inv(d)
        m = mat_mul(inv, rm)
        g = mat_mul(inv, rg)
        f = (inv[0] * a[0], inv[1] * a[1], inv[2] * a[0], inv[3] * a[1])
        n = (inv[0] * r[0], inv[1] * r[1], inv[2] * r[0], inv[3] * r[1])
        for e in range(4):
            fx[k, e] = f[e]
            gx[k, e] = g[e]
            ix[k, e] = inv[e]
            nx_[k, e] = n[e]
            ax[k, e] = a_all[e]
        return (g, m, mat_mul(a_all, f), add(k_all, mat_mul(a_all, m)))

    zero = jnp.zeros((SUB, LANES), F32)
    one = zero + 1.0
    unit = (one, zero, zero, one)
    none = (zero,) * 4
    kind = codes[0:1, :]
    top = (lax.broadcasted_iota(jnp.int32, (SUB, LANES), 0) == 0) & at_start
    sn, d0, d1 = rights(0)
    vented = (kind >= 1).astype(F32)
    opened = (kind == 1).astype(F32)
    r_first = tuple(jnp.where(top, vented * sn + opened * d, sn + d) for d in (d0, d1))
    half = depth // 2

    def plain(k):
        sn, d0, d1 = rights(k)
        return (sn + d0, sn + d1)

    def abreast(k, cs):
        return (step(k, cs[0], plain(k)), step(half + k, cs[1], plain(half + k)))

    fresh = (unit, none, unit, none)
    pair = (step(0, fresh, r_first), step(half, fresh, plain(half)))
    pair = chunked(1, half - 1, 2, abreast, pair)
    ends = []
    for n, (g, m, a_all, k_all) in enumerate(pair):
        end = (n + 1) * half - 1
        r = plain(end)
        rr = (r[0], r[0], r[1], r[1])
        a0 = lefts(n * half)
        aa = (a0[0], a0[0], a0[1], a0[1])
        sg = sigma(end)
        for c in range(2):
            halves[20 + 4 * n + c] = a0[c]
            halves[22 + 4 * n + c] = r[c]
        ends.append((
            tuple(x * y for x, y in zip(rr, g)),
            tuple(z + x * y for x, y, z in zip(rr, m, sg)),
            tuple(x * y for x, y in zip(aa, a_all)),
            tuple(x * y for x, y in zip(aa, k_all)),
        ))
    (lo, sg, a_all, k_all), (lo_end, sg_end, up, k_next) = ends
    sg = add(sg, k_next)
    inv = mat_inv(add(add(sg, lo), up))
    m, g, f = mat_mul(inv, sg), mat_mul(inv, lo), mat_mul(inv, up)
    lo_sub = mat_mul(lo_end, g)
    sg_sub = add(sg_end, mat_mul(lo_end, m))
    k_sub = add(k_all, mat_mul(a_all, m))
    a_sub = mat_mul(a_all, f)
    for e in range(4):
        halves[e] = f[e]
        halves[4 + e] = g[e]
        halves[8 + e] = inv[e]
        halves[12 + e] = lo_end[e]
        halves[16 + e] = a_all[e]
        edges[e] = lo_sub[e]
        edges[4 + e] = sg_sub[e]
        edges[8 + e] = a_sub[e]
        edges[12 + e] = k_sub[e]


def edge_rows(edges, first, n, s):
    return tuple(edges[first + e, pl.ds(s, 1), :] for e in range(n))


def x_chain_coefficients(edges, chain, pack, me):
    zrow = jnp.zeros((1, LANES), F32)
    orow = zrow + 1.0
    g, m = (orow, zrow, zrow, orow), (zrow,) * 4
    a_all, k_all = edge_rows(edges, 8, 4, 0), edge_rows(edges, 12, 4, 0)
    for s in range(SUB - 1):
        lo, up = edge_rows(edges, 0, 4, s), edge_rows(edges, 8, 4, s + 1)
        sg = add(edge_rows(edges, 4, 4, s), edge_rows(edges, 12, 4, s + 1))
        rm = add(sg, mat_mul(lo, m))
        rg = mat_mul(lo, g)
        inv = mat_inv(add(add(rm, up), rg))
        m, g, f = mat_mul(inv, rm), mat_mul(inv, rg), mat_mul(inv, up)
        for e in range(4):
            chain[s, pl.ds(e, 1), :] = f[e]
            chain[s, pl.ds(4 + e, 1), :] = g[e]
            chain[s, pl.ds(8 + e, 1), :] = inv[e]
            chain[s, pl.ds(12 + e, 1), :] = a_all[e]
        k_all = add(k_all, mat_mul(a_all, m))
        a_all = mat_mul(a_all, f)
    lo = edge_rows(edges, 0, 4, SUB - 1)
    sent = mat_mul(lo, g) + add(edge_rows(edges, 4, 4, SUB - 1), mat_mul(lo, m)) + a_all + k_all
    for e, row in enumerate(sent):
        pack[me, pl.ds(e, 1), :] = row


def x_values(weights, ix, nx_, ax, hx, halves, edges):
    depth = weights.shape[1] // SUB
    half = depth // 2

    def at(k):
        return tuple(weights[c, pl.ds(k, SUB, stride=depth), :] for c in range(2))

    def quad(ref, k):
        return tuple(ref[k, e] for e in range(4))

    def held(first, n):
        return tuple(halves[first + e] for e in range(n))

    def step(k, carry):
        h, v_all = carry
        base = mat_vec(quad(ix, k), at(k))
        n = quad(nx_, k)
        h = ((base[0] + n[0] * h[0]) + n[1] * h[1], (base[1] + n[2] * h[0]) + n[3] * h[1])
        for c in range(2):
            hx[k, c] = h[c]
        return h, add(v_all, mat_vec(quad(ax, k), h))

    def abreast(k, cs):
        return (step(k, cs[0]), step(half + k, cs[1]))

    zero = jnp.zeros((SUB, LANES), F32)
    fresh = ((zero, zero), (zero, zero))
    ends = []
    for n, (h, v_all) in enumerate(chunked(0, half - 1, 4, abreast, (fresh, fresh))):
        a0, r = held(20 + 4 * n, 2), held(22 + 4 * n, 2)
        w = at((n + 1) * half - 1)
        ends.append((tuple(w[c] + r[c] * h[c] for c in range(2)), tuple(a0[c] * v_all[c] for c in range(2))))
    (v, v_all), (v_end, v_next) = ends
    h = mat_vec(held(8, 4), add(v, v_next))
    v_end = add(v_end, mat_vec(held(12, 4), h))
    v_all = add(v_all, mat_vec(held(16, 4), h))
    for c in range(2):
        halves[28 + c] = h[c]
        edges[16 + c] = v_end[c]
        edges[18 + c] = v_all[c]


def x_chain_values(edges, chain, sums, pack, me):
    zrow = jnp.zeros((1, LANES), F32)
    h = (zrow, zrow)
    v_all = edge_rows(edges, 18, 2, 0)
    for s in range(SUB - 1):
        lo = edge_rows(edges, 0, 4, s)
        v = add(edge_rows(edges, 16, 2, s), edge_rows(edges, 18, 2, s + 1))
        inv = tuple(chain[s, pl.ds(8 + e, 1), :] for e in range(4))
        a_all = tuple(chain[s, pl.ds(12 + e, 1), :] for e in range(4))
        h = mat_vec(inv, add(v, mat_vec(lo, h)))
        for c in range(2):
            sums[s, pl.ds(c, 1), :] = h[c]
        v_all = add(v_all, mat_vec(a_all, h))
    lo = edge_rows(edges, 0, 4, SUB - 1)
    sent = add(edge_rows(edges, 16, 2, SUB - 1), mat_vec(lo, h)) + v_all
    for e in range(SUB):
        pack[me, pl.ds(e, 1), :] = sent[e] if e < len(sent) else zrow


def x_backward(nx, coefs, values, chain, sums, halves, fx, gx, hx, out, q_all, before, own):
    def row(ref, j, first, n):
        return tuple(ref[j, pl.ds(first + e, 1), :] for e in range(n))

    zrow = jnp.zeros((1, LANES), F32)
    orow = zrow + 1.0
    slack, h = (orow, zrow, zrow, orow), (zrow, zrow)
    factors = []
    for j in range(nx):
        lo, sg, v = row(coefs, j, 0, 4), row(coefs, j, 4, 4), row(values, j, 0, 2)
        up = (zrow,) * 4
        if j + 1 < nx:
            up = row(coefs, j + 1, 8, 4)
            sg = add(sg, row(coefs, j + 1, 12, 4))
            v = add(v, row(values, j + 1, 2, 2))
        t = add(sg, mat_mul(lo, slack))
        inv = mat_inv(add(t, up))
        slack = mat_mul(inv, t)
        h = mat_vec(inv, add(v, mat_vec(lo, h)))
        factors.append((mat_mul(inv, up), h))
    q = (zrow, zrow)
    for c in range(2):
        q_all[0, pl.ds(c, 1), :] = zrow
    for j in reversed(range(nx)):
        f, h = factors[j]
        q = add(mat_vec(f, q), h)
        for c in range(2):
            q_all[j + 1, pl.ds(c, 1), :] = q[c]
    me = lax.axis_index("xg")
    p = tuple(q_all[me, pl.ds(c, 1), :] for c in range(2))
    q = tuple(q_all[me + 1, pl.ds(c, 1), :] for c in range(2))
    for c in range(2):
        own[c, pl.ds(SUB - 1, 1), :] = q[c]
        before[c, pl.ds(0, 1), :] = p[c]
    for s in reversed(range(SUB - 1)):
        f = tuple(chain[s, pl.ds(e, 1), :] for e in range(4))
        g = tuple(chain[s, pl.ds(4 + e, 1), :] for e in range(4))
        h = tuple(sums[s, pl.ds(c, 1), :] for c in range(2))
        q = add(mat_vec(f, q), add(mat_vec(g, p), h))
        for c in range(2):
            own[c, pl.ds(s, 1), :] = q[c]
            before[c, pl.ds(s + 1, 1), :] = q[c]
    depth = out.shape[2] // SUB
    half = depth // 2
    prev = (before[0], before[1])
    x = (own[0], own[1])

    def held(first, n):
        return tuple(halves[first + e] for e in range(n))

    mid = add(mat_vec(held(0, 4), x), add(mat_vec(held(4, 4), prev), held(28, 2)))

    def put(k, x):
        for c in range(2):
            out[c, 0, pl.ds(k, SUB, stride=depth), :] = x[c]

    put(depth - 1, x)
    put(half - 1, mid)

    def solve(k, x, start):
        f = tuple(fx[k, e] for e in range(4))
        g = tuple(gx[k, e] for e in range(4))
        base = add(mat_vec(g, start), (hx[k, 0], hx[k, 1]))
        x = ((base[0] + f[0] * x[0]) + f[1] * x[1], (base[1] + f[2] * x[0]) + f[3] * x[1])
        put(k, x)
        return x

    def back(n, xs):
        return (solve(half - 2 - n, xs[0], prev), solve(depth - 2 - n, xs[1], mid))

    chunked(0, half - 1, 4, back, (mid, x))


def sends(axis, count, ref, send_sem, recv_sem):
    me = lax.axis_index(axis)
    return [
        pltpu.make_async_remote_copy(
            src_ref=ref.at[me],
            dst_ref=ref.at[me],
            send_sem=send_sem.at[k - 1],
            recv_sem=recv_sem.at[k - 1],
            device_id={axis: lax.rem(me + k, count)},
            device_id_type=pl.DeviceIdType.MESH,
        )
        for k in range(1, count)
    ]


def kernel(ny, nx, *refs):
    sources, out = refs[:10], refs[10]
    held = refs[11:21]
    (fy, gy, hy, left, right, rhs, first, y_packs, q_y, weights, fx, gx, ix, nx_, ax, hx, edges,
     chain, sums, x_coefs, x_vals, q_x, before, own, joint, halves,
     in_sem, y_send, y_recv, c_send, c_recv, v_send, v_recv) = refs[21:]
    cot, x_diff, x_speed, x_up, y_diff, y_speed, y_up, coupling, x_codes, y_codes = held
    loads = [pltpu.make_async_copy(s, d, in_sem.at[i]) for i, (s, d) in enumerate(zip(sources, held))]
    y_order, x_order = (5, 6, 4, 0, 9), (2, 3, 1, 7, 8)
    for i in y_order + x_order:
        loads[i].start()
    barrier = pltpu.get_barrier_semaphore()
    for axis, count in (("yd", ny), ("xg", nx)):
        for k in range(1, count):
            peer = lax.rem(lax.axis_index(axis) + k, count)
            pl.semaphore_signal(barrier, inc=1, device_id={axis: peer}, device_id_type=pl.DeviceIdType.MESH)
    for i in y_order:
        loads[i].wait()
    me_y, me_x = lax.axis_index("yd"), lax.axis_index("xg")
    y_forward(cot, y_diff, y_speed, y_up, y_codes, fy, gy, hy, y_packs.at[me_y], left, right, rhs, first, joint)
    pl.semaphore_wait(barrier, ny + nx - 2)
    y_copies = sends("yd", ny, y_packs, y_send, y_recv)
    for copy in y_copies:
        copy.start()
    for i in x_order:
        loads[i].wait()
    x_coefficients(x_diff, x_speed, x_up, coupling, x_codes, fx, gx, ix, nx_, ax, halves, edges)
    x_chain_coefficients(edges, chain, x_coefs, me_x)
    c_copies = sends("xg", nx, x_coefs, c_send, c_recv)
    for copy in c_copies:
        copy.start()
    for copy in y_copies:
        copy.wait()
    p, q = y_interfaces(ny, y_packs, q_y, fy.shape[1])
    y_backward(p, q, fy, gy, hy, joint, left, weights)
    x_values(weights, ix, nx_, ax, hx, halves, edges)
    x_chain_values(edges, chain, sums, x_vals, me_x)
    v_copies = sends("xg", nx, x_vals, v_send, v_recv)
    for copy in v_copies:
        copy.start()
    for copy in c_copies:
        copy.wait()
    for copy in v_copies:
        copy.wait()
    x_backward(nx, x_coefs, x_vals, chain, sums, halves, fx, gx, hx, out, q_x, before, own)


PIECES = 4


def hand_kernel(src, out, held, in_sem, out_sem):
    rows = src.shape[2] // (PIECES // 2)
    loads, stores = [], []
    for n in range(PIECES):
        where = (n % 2, 0, pl.ds(n // 2 * rows, rows))
        loads.append(pltpu.make_async_copy(src.at[where], held.at[n], in_sem.at[n]))
        stores.append(pltpu.make_async_copy(held.at[n], out.at[where], out_sem.at[n]))
    for copy in loads:
        copy.start()
    for load, store in zip(loads, stores):
        load.wait()
        store.start()
    for copy in stores:
        copy.wait()


def handed_on(block):
    return pl.pallas_call(
        hand_kernel,
        out_shape=jax.ShapeDtypeStruct(block.shape, block.dtype),
        in_specs=[pl.BlockSpec(memory_space=pl.ANY)],
        out_specs=pl.BlockSpec(memory_space=pl.ANY),
        scratch_shapes=[
            pltpu.VMEM((PIECES, block.shape[2] // (PIECES // 2), block.shape[3]), block.dtype),
            pltpu.SemaphoreType.DMA((PIECES,)),
            pltpu.SemaphoreType.DMA((PIECES,)),
        ],
        compiler_params=pltpu.CompilerParams(vmem_limit_bytes=61 * 1024 * 1024),
        name="hand_on",
    )(block)


def per_device(ny, nx, *args):
    rows_x, length = args[0].shape[2], args[0].shape[3]
    width = 2 * rows_x // LANES
    depth = rows_x // SUB
    tall = (length * width, LANES)
    deep = (length, width, LANES)
    quad = (depth, 4, SUB, LANES)
    shapes = [
        deep, deep, deep, tall, tall, tall, (3, width, LANES), (ny, 6, width, LANES), (ny + 1, width, LANES),
        (2, rows_x, LANES), quad, quad, quad, quad, quad, (depth, 2, SUB, LANES), (24, SUB, LANES),
        (SUB, 16, LANES), (SUB, SUB, LANES), (nx, 16, LANES), (nx, SUB, LANES), (nx + 1, SUB, LANES),
        (2, SUB, LANES), (2, SUB, LANES), (PARTS - 1, 3, width, LANES), (30, SUB, LANES),
    ]
    dma = pltpu.SemaphoreType.DMA
    solved = pl.pallas_call(
        functools.partial(kernel, ny, nx),
        out_shape=jax.ShapeDtypeStruct(args[0].shape, F32),
        in_specs=[pl.BlockSpec(memory_space=pl.ANY)] * len(args),
        out_specs=pl.BlockSpec(memory_space=pltpu.VMEM),
        scratch_shapes=[pltpu.VMEM(a.shape, a.dtype) for a in args]
        + [pltpu.VMEM(s, F32) for s in shapes]
        + [dma((len(args),)), dma((ny - 1,)), dma((ny - 1,)), dma((nx - 1,)), dma((nx - 1,)),
           dma((nx - 1,)), dma((nx - 1,))],
        compiler_params=pltpu.CompilerParams(
            collective_id=0, has_side_effects=True, vmem_limit_bytes=56 * 1024 * 1024
        ),
        name="adjoint_step",
    )(*args)
    return handed_on(solved)


def solution(mesh):
    body = functools.partial(per_device, mesh.shape["yd"], mesh.shape["xg"])
    return jax.shard_map(
        body,
        mesh=mesh,
        in_specs=(
            P(None, None, "xg", "yd"),
            P(None, None, "xg", "yd"),
            P(None, "xg", "yd"),
            P(None, "xg", "yd"),
            P(None, None, "xg", "yd"),
            P(None, "xg", "yd"),
            P(None, "xg", "yd"),
            P(None, None, "xg", "yd"),
            P(None, "yd"),
            P(None, "xg"),
        ),
        out_specs=P(None, None, "xg", "yd"),
        check_vma=False,
    )
```

```python
import functools

import jax
import jax.numpy as jnp
from jax import lax
from jax.experimental import pallas as pl
from jax.experimental.pallas import tpu as pltpu
from jax.sharding import PartitionSpec as P

LANES = 128
SUB = 8
PARTS = 4
F32 = jnp.float32


def mat_mul(p, q):
    return (
        p[0] * q[0] + p[1] * q[2],
        p[0] * q[1] + p[1] * q[3],
        p[2] * q[0] + p[3] * q[2],
        p[2] * q[1] + p[3] * q[3],
    )


def mat_vec(p, v):
    return (p[0] * v[0] + p[1] * v[1], p[2] * v[0] + p[3] * v[1])


def mat_inv(p):
    inv = 1.0 / (p[0] * p[3] - p[1] * p[2])
    return (p[3] * inv, -p[1] * inv, -p[2] * inv, p[0] * inv)


def add(p, q):
    return tuple(x + y for x, y in zip(p, q))


def chunked(lo, hi, unroll, body, carry):
    whole = (hi - lo) // unroll

    def group(step, c):
        for u in range(unroll):
            c = body(lo + step * unroll + u, c)
        return c

    carry = lax.fori_loop(0, whole, group, carry)
    for i in range(lo + whole * unroll, hi):
        carry = body(i, carry)
    return carry


def y_forward(cot, diff, speed, upwind, codes, f_out, g_out, h_out, pack, left, right, rhs, first, joint):
    rows_x, length = cot.shape[2], cot.shape[3]
    chunks = rows_x // LANES
    width = 2 * chunks
    boundary = lax.axis_index("yd") == 0
    for j in range(chunks):
        span = pl.ds(j * LANES, LANES)
        sp = speed[0, span, :]
        sm = sp * upwind[0, span, :].astype(F32)
        smt = sm.T
        snt = (sp - sm).T
        for c in range(2):
            slot = c * chunks + j
            df = diff[c, 0, span, :].T
            where = pl.ds(slot, length, stride=width)
            left[where, :] = smt + df
            right[where, :] = snt + df
            rhs[where, :] = cot[c, 0, span, :].T
            first[0, pl.ds(slot, 1), :] = snt[0:1, :]
            first[1, pl.ds(slot, 1), :] = df[0:1, :]
            first[2, pl.ds(slot, 1), :] = codes[0:1, span].astype(F32)

    def at(ref, i):
        return ref[pl.ds(pl.multiple_of(i * width, width), width), :]

    kind = first[2]
    edge = jnp.where(kind >= 0.5, first[0], 0.0) + jnp.where(jnp.abs(kind - 1.0) < 0.5, first[1], 0.0)
    r0 = jnp.where(boundary, edge, at(right, 0))
    right[pl.ds(0, width), :] = r0

    def step(i, carry):
        g, m, h, a_all, k_all, v_all = carry
        a = at(left, i + 1)
        r = at(right, i)
        rm = 1.0 + r * m
        rg = r * g
        inv = 1.0 / ((rm + a) + rg)
        m = rm * inv
        g = rg * inv
        h = (at(rhs, i) + r * h) * inv
        f = a * inv
        f_out[i] = f
        g_out[i] = g
        h_out[i] = h
        return (g, m, h, a_all * f, k_all + a_all * m, v_all + a_all * h)

    zero = jnp.zeros((width, LANES), F32)
    one = zero + 1.0
    seg = length // PARTS

    def abreast(i, carries):
        return tuple(step(n * seg + i, c) for n, c in enumerate(carries))

    start = ((one, zero, zero, one, zero, zero),) * PARTS
    parts = []
    for n, (g, m, h, a_all, k_all, v_all) in enumerate(chunked(0, seg - 1, 4, abreast, start)):
        r = at(right, (n + 1) * seg - 1)
        a0 = at(left, n * seg)
        v = at(rhs, (n + 1) * seg - 1) + r * h
        parts.append((r * g, 1.0 + r * m, v, a0 * a_all, a0 * k_all, a0 * v_all))
    g, m, h = one, zero, zero
    a_all, k_all, v_all = parts[0][3:]
    for n in range(PARTS - 1):
        lo, sg, v = parts[n][:3]
        up, k_next, v_next = parts[n + 1][3:]
        rm = (sg + k_next) + lo * m
        rg = lo * g
        inv = 1.0 / ((rm + up) + rg)
        m = rm * inv
        g = rg * inv
        h = ((v + v_next) + lo * h) * inv
        f = up * inv
        joint[n, 0] = f
        joint[n, 1] = g
        joint[n, 2] = h
        k_all = k_all + a_all * m
        v_all = v_all + a_all * h
        a_all = a_all * f
    lo, sg, v = parts[-1][:3]
    for e, value in enumerate((lo * g, sg + lo * m, v + lo * h, a_all, k_all, v_all)):
        pack[e] = value


def y_interfaces(ny, packs, q_all, width):
    zero = jnp.zeros((width, LANES), F32)
    slack, h = zero + 1.0, zero
    factors = []
    for j in range(ny):
        lo, sg, v = packs[j, 0], packs[j, 1], packs[j, 2]
        up = zero
        if j + 1 < ny:
            up = packs[j + 1, 3]
            sg = sg + packs[j + 1, 4]
            v = v + packs[j + 1, 5]
        t = sg + lo * slack
        inv = 1.0 / (t + up)
        slack = t * inv
        h = (v + lo * h) * inv
        factors.append((up * inv, h))
    q = zero
    for j in reversed(range(ny)):
        f, h = factors[j]
        q = f * q + h
        q_all[j + 1] = q
    q_all[0] = zero
    me = lax.axis_index("yd")
    return q_all[me], q_all[me + 1]


def y_backward(p, q, fy, gy, hy, joint, lines, weights):
    length, width = fy.shape[0], fy.shape[1]

    def put(i, value):
        lines[pl.ds(pl.multiple_of(i * width, width), width), :] = value

    seg = length // PARTS
    ends = [q]
    for n in reversed(range(PARTS - 1)):
        ends.insert(0, joint[n, 0] * ends[0] + (joint[n, 1] * p + joint[n, 2]))
    starts = [p] + ends[:-1]
    for n in range(PARTS):
        put((n + 1) * seg - 1, ends[n])

    def back(k, ws):
        done = []
        for n, w in enumerate(ws):
            i = (n + 1) * seg - 2 - k
            w = fy[i] * w + (gy[i] * starts[n] + hy[i])
            put(i, w)
            done.append(w)
        return tuple(done)

    chunked(0, seg - 1, 4, back, tuple(ends))
    chunks = width // 2
    for c in range(2):
        for j in range(chunks):
            block = lines[pl.ds(c * chunks + j, length, stride=width), :]
            weights[c, pl.ds(j * LANES, LANES), :] = block.T


def x_coefficients(diff, speed, upwind, coupling, codes, fx, gx, ix, nx_, ax, halves, edges):
    depth = diff.shape[2] // SUB
    at_start = lax.axis_index("xg") == 0

    def rows(k):
        return pl.ds(k, SUB, stride=depth)

    def lefts(k):
        sm = speed[0, rows(k), :] * upwind[0, rows(k), :].astype(F32)
        return (sm + diff[0, 0, rows(k), :], sm + diff[1, 0, rows(k), :])

    def rights(k):
        sp = speed[0, rows(k), :]
        sn = sp - sp * upwind[0, rows(k), :].astype(F32)
        return (sn, diff[0, 0, rows(k), :], diff[1, 0, rows(k), :])

    def sigma(k):
        return (
            1.0 + 0.5 * coupling[0, 0, rows(k), :],
            0.5 * coupling[2, 0, rows(k), :],
            0.5 * coupling[1, 0, rows(k), :],
            1.0 + 0.5 * coupling[3, 0, rows(k), :],
        )

    def step(k, carry, r):
        g, m, a_all, k_all = carry
        a = lefts(k + 1)
        sg = sigma(k)
        rm = (sg[0] + r[0] * m[0], sg[1] + r[0] * m[1], sg[2] + r[1] * m[2], sg[3] + r[1] * m[3])
        rg = (r[0] * g[0], r[0] * g[1], r[1] * g[2], r[1] * g[3])
        d = (rm[0] + a[0] + rg[0], rm[1] + rg[1], rm[2] + rg[2], rm[3] + a[1] + rg[3])
        inv = mat_inv(d)
        m = mat_mul(inv, rm)
        g = mat_mul(inv, rg)
        f = (inv[0] * a[0], inv[1] * a[1], inv[2] * a[0], inv[3] * a[1])
        n = (inv[0] * r[0], inv[1] * r[1], inv[2] * r[0], inv[3] * r[1])
        for e in range(4):
            fx[k, e] = f[e]
            gx[k, e] = g[e]
            ix[k, e] = inv[e]
            nx_[k, e] = n[e]
            ax[k, e] = a_all[e]
        return (g, m, mat_mul(a_all, f), add(k_all, mat_mul(a_all, m)))

    zero = jnp.zeros((SUB, LANES), F32)
    one = zero + 1.0
    unit = (one, zero, zero, one)
    none = (zero,) * 4
    kind = codes[0:1, :]
    top = (lax.broadcasted_iota(jnp.int32, (SUB, LANES), 0) == 0) & at_start
    sn, d0, d1 = rights(0)
    vented = (kind >= 1).astype(F32)
    opened = (kind == 1).astype(F32)
    r_first = tuple(jnp.where(top, vented * sn + opened * d, sn + d) for d in (d0, d1))
    half = depth // 2

    def plain(k):
        sn, d0, d1 = rights(k)
        return (sn + d0, sn + d1)

    def abreast(k, cs):
        return (step(k, cs[0], plain(k)), step(half + k, cs[1], plain(half + k)))

    fresh = (unit, none, unit, none)
    pair = (step(0, fresh, r_first), step(half, fresh, plain(half)))
    pair = chunked(1, half - 1, 2, abreast, pair)
    ends = []
    for n, (g, m, a_all, k_all) in enumerate(pair):
        end = (n + 1) * half - 1
        r = plain(end)
        rr = (r[0], r[0], r[1], r[1])
        a0 = lefts(n * half)
        aa = (a0[0], a0[0], a0[1], a0[1])
        sg = sigma(end)
        for c in range(2):
            halves[20 + 4 * n + c] = a0[c]
            halves[22 + 4 * n + c] = r[c]
        ends.append((
            tuple(x * y for x, y in zip(rr, g)),
            tuple(z + x * y for x, y, z in zip(rr, m, sg)),
            tuple(x * y for x, y in zip(aa, a_all)),
            tuple(x * y for x, y in zip(aa, k_all)),
        ))
    (lo, sg, a_all, k_all), (lo_end, sg_end, up, k_next) = ends
    sg = add(sg, k_next)
    inv = mat_inv(add(add(sg, lo), up))
    m, g, f = mat_mul(inv, sg), mat_mul(inv, lo), mat_mul(inv, up)
    lo_sub = mat_mul(lo_end, g)
    sg_sub = add(sg_end, mat_mul(lo_end, m))
    k_sub = add(k_all, mat_mul(a_all, m))
    a_sub = mat_mul(a_all, f)
    for e in range(4):
        halves[e] = f[e]
        halves[4 + e] = g[e]
        halves[8 + e] = inv[e]
        halves[12 + e] = lo_end[e]
        halves[16 + e] = a_all[e]
        edges[e] = lo_sub[e]
        edges[4 + e] = sg_sub[e]
        edges[8 + e] = a_sub[e]
        edges[12 + e] = k_sub[e]


def edge_rows(edges, first, n, s):
    return tuple(edges[first + e, pl.ds(s, 1), :] for e in range(n))


def x_chain_coefficients(edges, chain, pack, me):
    zrow = jnp.zeros((1, LANES), F32)
    orow = zrow + 1.0
    g, m = (orow, zrow, zrow, orow), (zrow,) * 4
    a_all, k_all = edge_rows(edges, 8, 4, 0), edge_rows(edges, 12, 4, 0)
    for s in range(SUB - 1):
        lo, up = edge_rows(edges, 0, 4, s), edge_rows(edges, 8, 4, s + 1)
        sg = add(edge_rows(edges, 4, 4, s), edge_rows(edges, 12, 4, s + 1))
        rm = add(sg, mat_mul(lo, m))
        rg = mat_mul(lo, g)
        inv = mat_inv(add(add(rm, up), rg))
        m, g, f = mat_mul(inv, rm), mat_mul(inv, rg), mat_mul(inv, up)
        for e in range(4):
            chain[s, pl.ds(e, 1), :] = f[e]
            chain[s, pl.ds(4 + e, 1), :] = g[e]
            chain[s, pl.ds(8 + e, 1), :] = inv[e]
            chain[s, pl.ds(12 + e, 1), :] = a_all[e]
        k_all = add(k_all, mat_mul(a_all, m))
        a_all = mat_mul(a_all, f)
    lo = edge_rows(edges, 0, 4, SUB - 1)
    sent = mat_mul(lo, g) + add(edge_rows(edges, 4, 4, SUB - 1), mat_mul(lo, m)) + a_all + k_all
    for e, row in enumerate(sent):
        pack[me, pl.ds(e, 1), :] = row


def x_values(weights, ix, nx_, ax, hx, halves, edges):
    depth = weights.shape[1] // SUB
    half = depth // 2

    def at(k):
        return tuple(weights[c, pl.ds(k, SUB, stride=depth), :] for c in range(2))

    def quad(ref, k):
        return tuple(ref[k, e] for e in range(4))

    def held(first, n):
        return tuple(halves[first + e] for e in range(n))

    def step(k, carry):
        h, v_all = carry
        base = mat_vec(quad(ix, k), at(k))
        n = quad(nx_, k)
        h = ((base[0] + n[0] * h[0]) + n[1] * h[1], (base[1] + n[2] * h[0]) + n[3] * h[1])
        for c in range(2):
            hx[k, c] = h[c]
        return h, add(v_all, mat_vec(quad(ax, k), h))

    def abreast(k, cs):
        return (step(k, cs[0]), step(half + k, cs[1]))

    zero = jnp.zeros((SUB, LANES), F32)
    fresh = ((zero, zero), (zero, zero))
    ends = []
    for n, (h, v_all) in enumerate(chunked(0, half - 1, 4, abreast, (fresh, fresh))):
        a0, r = held(20 + 4 * n, 2), held(22 + 4 * n, 2)
        w = at((n + 1) * half - 1)
        ends.append((tuple(w[c] + r[c] * h[c] for c in range(2)), tuple(a0[c] * v_all[c] for c in range(2))))
    (v, v_all), (v_end, v_next) = ends
    h = mat_vec(held(8, 4), add(v, v_next))
    v_end = add(v_end, mat_vec(held(12, 4), h))
    v_all = add(v_all, mat_vec(held(16, 4), h))
    for c in range(2):
        halves[28 + c] = h[c]
        edges[16 + c] = v_end[c]
        edges[18 + c] = v_all[c]


def x_chain_values(edges, chain, sums, pack, me):
    zrow = jnp.zeros((1, LANES), F32)
    h = (zrow, zrow)
    v_all = edge_rows(edges, 18, 2, 0)
    for s in range(SUB - 1):
        lo = edge_rows(edges, 0, 4, s)
        v = add(edge_rows(edges, 16, 2, s), edge_rows(edges, 18, 2, s + 1))
        inv = tuple(chain[s, pl.ds(8 + e, 1), :] for e in range(4))
        a_all = tuple(chain[s, pl.ds(12 + e, 1), :] for e in range(4))
        h = mat_vec(inv, add(v, mat_vec(lo, h)))
        for c in range(2):
            sums[s, pl.ds(c, 1), :] = h[c]
        v_all = add(v_all, mat_vec(a_all, h))
    lo = edge_rows(edges, 0, 4, SUB - 1)
    sent = add(edge_rows(edges, 16, 2, SUB - 1), mat_vec(lo, h)) + v_all
    for e in range(SUB):
        pack[me, pl.ds(e, 1), :] = sent[e] if e < len(sent) else zrow


def x_backward(nx, coefs, values, v_copies, chain, sums, halves, fx, gx, hx, out, q_all, before, own):
    def row(ref, j, first, n):
        return tuple(ref[j, pl.ds(first + e, 1), :] for e in range(n))

    zrow = jnp.zeros((1, LANES), F32)
    orow = zrow + 1.0
    slack, h = (orow, zrow, zrow, orow), (zrow, zrow)
    solvers, factors = [], []
    for j in range(nx):
        lo, sg = row(coefs, j, 0, 4), row(coefs, j, 4, 4)
        up = (zrow,) * 4
        if j + 1 < nx:
            up = row(coefs, j + 1, 8, 4)
            sg = add(sg, row(coefs, j + 1, 12, 4))
        t = add(sg, mat_mul(lo, slack))
        inv = mat_inv(add(t, up))
        slack = mat_mul(inv, t)
        solvers.append((lo, inv, mat_mul(inv, up)))
    for copy in v_copies:
        copy.wait()
    for j, (lo, inv, f) in enumerate(solvers):
        v = row(values, j, 0, 2)
        if j + 1 < nx:
            v = add(v, row(values, j + 1, 2, 2))
        h = mat_vec(inv, add(v, mat_vec(lo, h)))
        factors.append((f, h))
    q = (zrow, zrow)
    for c in range(2):
        q_all[0, pl.ds(c, 1), :] = zrow
    for j in reversed(range(nx)):
        f, h = factors[j]
        q = add(mat_vec(f, q), h)
        for c in range(2):
            q_all[j + 1, pl.ds(c, 1), :] = q[c]
    me = lax.axis_index("xg")
    p = tuple(q_all[me, pl.ds(c, 1), :] for c in range(2))
    q = tuple(q_all[me + 1, pl.ds(c, 1), :] for c in range(2))
    for c in range(2):
        own[c, pl.ds(SUB - 1, 1), :] = q[c]
        before[c, pl.ds(0, 1), :] = p[c]
    for s in reversed(range(SUB - 1)):
        f = tuple(chain[s, pl.ds(e, 1), :] for e in range(4))
        g = tuple(chain[s, pl.ds(4 + e, 1), :] for e in range(4))
        h = tuple(sums[s, pl.ds(c, 1), :] for c in range(2))
        q = add(mat_vec(f, q), add(mat_vec(g, p), h))
        for c in range(2):
            own[c, pl.ds(s, 1), :] = q[c]
            before[c, pl.ds(s + 1, 1), :] = q[c]
    depth = out.shape[2] // SUB
    half = depth // 2
    prev = (before[0], before[1])
    x = (own[0], own[1])

    def held(first, n):
        return tuple(halves[first + e] for e in range(n))

    mid = add(mat_vec(held(0, 4), x), add(mat_vec(held(4, 4), prev), held(28, 2)))

    def put(k, x):
        for c in range(2):
            out[c, 0, pl.ds(k, SUB, stride=depth), :] = x[c]

    put(depth - 1, x)
    put(half - 1, mid)

    def solve(k, x, start):
        f = tuple(fx[k, e] for e in range(4))
        g = tuple(gx[k, e] for e in range(4))
        base = add(mat_vec(g, start), (hx[k, 0], hx[k, 1]))
        x = ((base[0] + f[0] * x[0]) + f[1] * x[1], (base[1] + f[2] * x[0]) + f[3] * x[1])
        put(k, x)
        return x

    def back(n, xs):
        return (solve(half - 2 - n, xs[0], prev), solve(depth - 2 - n, xs[1], mid))

    chunked(0, half - 1, 4, back, (mid, x))


def sends(axis, count, ref, send_sem, recv_sem):
    me = lax.axis_index(axis)
    return [
        pltpu.make_async_remote_copy(
            src_ref=ref.at[me],
            dst_ref=ref.at[me],
            send_sem=send_sem.at[k - 1],
            recv_sem=recv_sem.at[k - 1],
            device_id={axis: lax.rem(me + k, count)},
            device_id_type=pl.DeviceIdType.MESH,
        )
        for k in range(1, count)
    ]


def kernel(ny, nx, *refs):
    sources, out = refs[:10], refs[10]
    held = refs[11:21]
    (fy, gy, hy, left, right, rhs, first, y_packs, q_y, weights, fx, gx, ix, nx_, ax, hx, edges,
     chain, sums, x_coefs, x_vals, q_x, before, own, joint, halves,
     in_sem, y_send, y_recv, c_send, c_recv, v_send, v_recv) = refs[21:]
    cot, x_diff, x_speed, x_up, y_diff, y_speed, y_up, coupling, x_codes, y_codes = held
    loads = [pltpu.make_async_copy(s, d, in_sem.at[i]) for i, (s, d) in enumerate(zip(sources, held))]
    y_order, x_order = (5, 6, 4, 0, 9), (2, 3, 1, 7, 8)
    for i in y_order + x_order:
        loads[i].start()
    barrier = pltpu.get_barrier_semaphore()
    for axis, count in (("yd", ny), ("xg", nx)):
        for k in range(1, count):
            peer = lax.rem(lax.axis_index(axis) + k, count)
            pl.semaphore_signal(barrier, inc=1, device_id={axis: peer}, device_id_type=pl.DeviceIdType.MESH)
    for i in y_order:
        loads[i].wait()
    me_y, me_x = lax.axis_index("yd"), lax.axis_index("xg")
    y_forward(cot, y_diff, y_speed, y_up, y_codes, fy, gy, hy, y_packs.at[me_y], left, right, rhs, first, joint)
    pl.semaphore_wait(barrier, ny + nx - 2)
    y_copies = sends("yd", ny, y_packs, y_send, y_recv)
    for copy in y_copies:
        copy.start()
    for i in x_order:
        loads[i].wait()
    x_coefficients(x_diff, x_speed, x_up, coupling, x_codes, fx, gx, ix, nx_, ax, halves, edges)
    x_chain_coefficients(edges, chain, x_coefs, me_x)
    c_copies = sends("xg", nx, x_coefs, c_send, c_recv)
    for copy in c_copies:
        copy.start()
    for copy in y_copies:
        copy.wait()
    p, q = y_interfaces(ny, y_packs, q_y, fy.shape[1])
    y_backward(p, q, fy, gy, hy, joint, left, weights)
    x_values(weights, ix, nx_, ax, hx, halves, edges)
    x_chain_values(edges, chain, sums, x_vals, me_x)
    v_copies = sends("xg", nx, x_vals, v_send, v_recv)
    for copy in v_copies:
        copy.start()
    for copy in c_copies:
        copy.wait()
    x_backward(nx, x_coefs, x_vals, v_copies, chain, sums, halves, fx, gx, hx, out, q_x, before, own)


def per_device(ny, nx, *args):
    rows_x, length = args[0].shape[2], args[0].shape[3]
    width = 2 * rows_x // LANES
    depth = rows_x // SUB
    tall = (length * width, LANES)
    deep = (length, width, LANES)
    quad = (depth, 4, SUB, LANES)
    shapes = [
        deep, deep, deep, tall, tall, tall, (3, width, LANES), (ny, 6, width, LANES), (ny + 1, width, LANES),
        (2, rows_x, LANES), quad, quad, quad, quad, quad, (depth, 2, SUB, LANES), (24, SUB, LANES),
        (SUB, 16, LANES), (SUB, SUB, LANES), (nx, 16, LANES), (nx, SUB, LANES), (nx + 1, SUB, LANES),
        (2, SUB, LANES), (2, SUB, LANES), (PARTS - 1, 3, width, LANES), (30, SUB, LANES),
    ]
    dma = pltpu.SemaphoreType.DMA
    return pl.pallas_call(
        functools.partial(kernel, ny, nx),
        out_shape=jax.ShapeDtypeStruct(args[0].shape, F32),
        in_specs=[pl.BlockSpec(memory_space=pl.ANY)] * len(args),
        out_specs=pl.BlockSpec(memory_space=pltpu.VMEM),
        scratch_shapes=[pltpu.VMEM(a.shape, a.dtype) for a in args]
        + [pltpu.VMEM(s, F32) for s in shapes]
        + [dma((len(args),)), dma((ny - 1,)), dma((ny - 1,)), dma((nx - 1,)), dma((nx - 1,)),
           dma((nx - 1,)), dma((nx - 1,))],
        compiler_params=pltpu.CompilerParams(
            collective_id=0, has_side_effects=True, vmem_limit_bytes=56 * 1024 * 1024
        ),
        name="adjoint_step",
    )(*args)


def solution(mesh):
    body = functools.partial(per_device, mesh.shape["yd"], mesh.shape["xg"])
    return jax.shard_map(
        body,
        mesh=mesh,
        in_specs=(
            P(None, None, "xg", "yd"),
            P(None, None, "xg", "yd"),
            P(None, "xg", "yd"),
            P(None, "xg", "yd"),
            P(None, None, "xg", "yd"),
            P(None, "xg", "yd"),
            P(None, "xg", "yd"),
            P(None, None, "xg", "yd"),
            P(None, "yd"),
            P(None, "xg"),
        ),
        out_specs=P(None, None, "xg", "yd"),
        check_vma=False,
    )
```
